512 devices in a mesh: dp: 16 (over y, x_hi), seq: 32 (over x_lo, z, core).
Axes of the slice: x: 4 (x_hi: 2, x_lo: 2; x = x_hi * 2 + x_lo), y: 8, z: 8, core: 2. Of those that a mesh axis runs over, the one named last changes fastest.
Arguments:
- queries: bfloat16 [32, 32, 128, 1152], P('dp', 'seq'), may hold values from -15 to 15
- key_states: bfloat16 [32, 32, 128, 1152], P('dp', 'seq'), may hold values from -8 to 8
- value_states: bfloat16 [32, 32, 128, 1152], P('dp', 'seq'), may hold values from -6 to 6
- gate_vector: float32 [32, 1152], P('dp'), may hold values from 0.5 to 2
- out_weight: bfloat16 [1152, 1152], P('seq'), may hold values from -0.1875 to 0.1875
- cotangent: bfloat16 [32, 32, 128, 1152], P('dp', None, 'seq'), may hold values from -6 to 6
Outputs:
- branch: bfloat16 [32, 32, 128, 1152], P('dp', None, 'seq')
- grad_query: bfloat16 [32, 32, 128, 1152], P('dp', 'seq')
- grad_key: bfloat16 [32, 32, 128, 1152], P('dp', 'seq')
- grad_value: bfloat16 [32, 32, 128, 1152], P('dp', 'seq')
- grad_weight: float32 [1152, 1152], P('seq')
The draws below stay inside these ranges and needn't reach their ends.
All inputs are finite; a program needn't handle non-finite values.
Results may differ from the reference program's by a relative error of at most 0.023.
Values may be sent and summed in bfloat16 or wider, within the bound.
A program may use at most 64 MiB of HBM per device.

```python
import math
import jax
import jax.numpy as jnp
from jax import lax

D = 1152
HEADS = 16
HEAD_DIM = 72
CLIP_DEV = 2
PA_DEV = 4
CLIPS = 32
FRAMES = 32
PATCHES = 128
N_DP = 16
N_SEQ = 32


def scaled_noise(scale_key, fresh_noise):
    row_scale = jnp.exp(jax.random.uniform(scale_key, (CLIPS, FRAMES, PATCHES, HEADS, 1), jnp.float32, math.log(0.5), math.log(2.0)))
    return (fresh_noise * row_scale).reshape(CLIPS, FRAMES // 2, 2, PATCHES, D)


def draw_queries(key, part):
    key = jax.random.fold_in(key, 11)
    scale_key, noise_key = jax.random.split(key)
    heads_shape = (CLIPS, FRAMES, PATCHES, HEADS, HEAD_DIM)
    fresh_noise = jax.random.truncated_normal(noise_key, -4.0, 4.0, heads_shape, jnp.float32)
    drawn = scaled_noise(scale_key, fresh_noise)
    return drawn.reshape(CLIPS, FRAMES, PATCHES, D).astype(jnp.bfloat16)


def draw_key_states(key, part):
    key = jax.random.fold_in(key, 12)
    scale_key, noise_key = jax.random.split(key)
    heads_shape = (CLIPS, FRAMES, PATCHES, HEADS, HEAD_DIM)
    fresh_noise = jax.random.truncated_normal(noise_key, -4.0, 4.0, heads_shape, jnp.float32)
    drawn = scaled_noise(scale_key, fresh_noise)
    return drawn.reshape(CLIPS, FRAMES, PATCHES, D).astype(jnp.bfloat16)


def raised(result, key, source, target, blocks, factor):
    def block_of(dim):
        return (jnp.arange(result.shape[dim]) // (result.shape[dim] // blocks)).reshape((-1,) + (1,) * (result.ndim - 1 - dim))

    near = jax.random.permutation(key, blocks)[block_of(target)]
    far = (block_of(target) + blocks // 2) % blocks
    return jnp.where((block_of(source) == near) | (block_of(source) == far), factor * result, result)


def block_levels(rng, shape, shards, low, top_value):
    def one(axis_at, blocks):
        steps = jax.random.uniform(jax.random.fold_in(jax.random.fold_in(rng, 6), axis_at), (blocks,), jnp.float32, low / len(shards), top_value / len(shards))
        return jnp.repeat(jnp.exp(steps), shape[axis_at] // blocks).reshape((-1,) + (1,) * (len(shape) - axis_at - 1))

    gain = one(*shards[0])
    for cut in shards[1:]:
        gain = gain * one(*cut)
    return gain


def gaussian(own_key, shape, deviation, reach, cuts=(), dtype=jnp.bfloat16):
    drawn = jax.random.normal(own_key, shape, jnp.float32) * deviation
    if len(cuts) > 0:
        drawn = block_levels(own_key, shape, cuts, -0.22, 0.18) * drawn
    return jnp.clip(drawn, min=-reach, max=reach).astype(dtype)


def bell_draw_with(rng, dims, deviation, reach, cuts, heavy, kind=jnp.bfloat16):
    values = deviation * jax.random.normal(rng, dims, jnp.float32)
    if cuts:
        values = values * block_levels(rng, dims, cuts, -0.22, 0.18)
    return jnp.clip(raised(values, jax.random.fold_in(rng, 3), *heavy), -reach, reach).astype(kind)


def setup_inputs(seed: int = 0) -> dict:
    splits = jax.random.split(jax.random.key(seed), 7)
    return {
        "queries": draw_queries(jax.random.fold_in(splits[6], 71), 0),
        "key_states": draw_key_states(jax.random.fold_in(splits[6], 71), 0),
        "value_states": gaussian(splits[2], (CLIPS, FRAMES, PATCHES, D), 1.0, 6.0, ((0, 16), (1, 32))),
        "gate_vector": jnp.clip(jnp.exp(math.log(2.0) - 1.3862944 * jax.random.uniform(splits[3], (CLIPS, D), jnp.float32) ** block_levels(splits[3], (CLIPS, D), ((0, 16),), -0.2, 0.2)), 0.5, 2.0),
        "out_weight": gaussian(splits[4], (D, D), D ** -0.5, 0.1875, ((0, 32),)),
        "cotangent": bell_draw_with(splits[5], (CLIPS, FRAMES, PATCHES, D), 1.0, 6.0, ((0, 16), (2, 32)), (2, 3, 32, 2.75)),
    }


def split_heads(tensor):
    return tensor.reshape(tensor.shape[:-1] + (HEADS, HEAD_DIM)).astype(jnp.float32)

def softmax_weights(queries, key_states):
    scaling = 1.0 / math.sqrt(HEAD_DIM)
    scores = jnp.einsum('cfxhd,cgxhd->cxhfg', split_heads(queries), split_heads(key_states)) * scaling
    return jax.nn.softmax(scores, axis=-1)

def attend(queries, key_states, value_states):
    weights = softmax_weights(queries, key_states).astype(jnp.bfloat16)
    heads_out = jnp.einsum('cxhfg,cgxhd->cfxhd', weights.astype(jnp.float32), split_heads(value_states))
    return heads_out.reshape(queries.shape).astype(jnp.bfloat16)

def attend_back(queries, key_states, value_states, attended_grad):
    scaling = 1.0 / math.sqrt(HEAD_DIM)
    probability = softmax_weights(queries, key_states)
    weights = probability.astype(jnp.bfloat16).astype(jnp.float32)
    grad_heads = split_heads(attended_grad)
    weight_grad = jnp.einsum('cfxhd,cgxhd->cxhfg', grad_heads, split_heads(value_states))
    centred = weight_grad - lax.optimization_barrier(jnp.sum(probability * weight_grad, axis=-1, keepdims=True))
    score_grad = (probability * centred * scaling).astype(jnp.bfloat16).astype(jnp.float32)
    query_grad = jnp.einsum('cxhfg,cgxhd->cfxhd', score_grad, split_heads(key_states))
    key_grad = jnp.einsum('cxhfg,cfxhd->cgxhd', score_grad, split_heads(queries))
    value_grad = jnp.einsum('cxhfg,cfxhd->cgxhd', weights, grad_heads)
    return tuple((tensor.reshape(queries.shape).astype(jnp.bfloat16) for tensor in (query_grad, key_grad, value_grad)))

def reference(queries, key_states, value_states, gate_vector, out_weight, cotangent):
    inverse_root = 1.0 / math.sqrt(CLIPS * FRAMES * PATCHES)

    def grouped(tensor):
        return tensor.reshape((N_DP, CLIP_DEV) + tensor.shape[1:])

    def by_blocks(tensor):
        return tensor.reshape(CLIP_DEV, FRAMES, N_SEQ, PA_DEV, D).transpose(2, 0, 1, 3, 4).reshape(N_SEQ, -1, D)

    def one_group(running, pieces):
        group_query, group_key, group_value, group_gate, group_cot = pieces
        attended = attend(group_query, group_key, group_value)
        projected = jnp.dot(attended.reshape(-1, D), out_weight.T, preferred_element_type=jnp.float32)
        gate_wide = group_gate[:, None, None, :]
        branch = (gate_wide * projected.reshape(attended.shape)).astype(jnp.bfloat16)
        mixed_grad = (gate_wide * group_cot.astype(jnp.float32)).astype(jnp.bfloat16)
        attended_grad = jnp.dot(mixed_grad.reshape(-1, D), out_weight, preferred_element_type=jnp.float32)
        attended_grad = attended_grad.astype(jnp.bfloat16).reshape(attended.shape)
        query_grad, key_grad, value_grad = attend_back(group_query, group_key, group_value, attended_grad)

        def one_block(partial_sum, blocks):
            block_term = lax.dot_general(blocks[1], blocks[0], (((0,), (0,)), ((), ())), preferred_element_type=jnp.float32) * inverse_root
            rounded = lax.optimization_barrier(block_term.astype(jnp.bfloat16))
            return (partial_sum + rounded.astype(jnp.float32), None)
        seq_total, _ = lax.scan(one_block, jnp.zeros((D, D), jnp.float32), (by_blocks(attended), by_blocks(mixed_grad)))
        return (running + seq_total, (branch, query_grad, key_grad, value_grad))
    inputs = tuple((grouped(tensor) for tensor in (queries, key_states, value_states, gate_vector, cotangent)))
    grad_weight, stacked = lax.scan(one_group, jnp.zeros((D, D), jnp.float32), inputs)
    branch, grad_query, grad_key, grad_value = (tensor.reshape((CLIPS,) + tensor.shape[2:]) for tensor in stacked)
    return (branch, grad_query, grad_key, grad_value, grad_weight)
```

```python
import functools
import math

import jax
import jax.numpy as jnp
from jax import lax
from jax.experimental import pallas as pl
from jax.experimental.pallas import tpu as pltpu
from jax.sharding import PartitionSpec as P

HEADS = 16


MESH = pl.DeviceIdType.MESH


def exchange_kernel(count, peers, *refs):
    ins, outs = refs[:count], refs[count : 2 * count]
    send_sem, recv_sem, own_sem = refs[2 * count :]
    dp, me = lax.axis_index("dp"), lax.axis_index("seq")
    barrier = pltpu.get_barrier_semaphore()

    def greet(step, carry):
        pl.semaphore_signal(
            barrier, inc=1, device_id=(dp, lax.rem(me + step, peers)), device_id_type=MESH
        )
        return carry

    lax.fori_loop(1, peers, greet, 0)
    pl.semaphore_wait(barrier, peers - 1)
    for t in range(count):

        def send(step, carry):
            target = lax.rem(me + step, peers)
            pltpu.make_async_remote_copy(
                src_ref=ins[t].at[target],
                dst_ref=outs[t].at[me],
                send_sem=send_sem.at[t],
                recv_sem=recv_sem.at[t],
                device_id=(dp, target),
                device_id_type=MESH,
            ).start()
            return carry

        lax.fori_loop(1, peers, send, 0)
        pltpu.make_async_copy(ins[t].at[me], outs[t].at[me], own_sem.at[t]).start()
    for t in range(count):
        pltpu.make_async_copy(ins[t].at[me], outs[t].at[me], own_sem.at[t]).wait()
        whole = pltpu.make_async_remote_copy(
            src_ref=ins[t].at[pl.ds(0, peers - 1)],
            dst_ref=outs[t].at[pl.ds(0, peers - 1)],
            send_sem=send_sem.at[t],
            recv_sem=recv_sem.at[t],
            device_id=(dp, lax.rem(me + 1, peers)),
            device_id_type=MESH,
        )
        whole.wait_send()
        whole.wait_recv()


def exchange(tensors, collective_id):
    count, peers = len(tensors), tensors[0].shape[0]
    whole = [pl.BlockSpec(memory_space=pltpu.VMEM)] * count
    return pl.pallas_call(
        functools.partial(exchange_kernel, count, peers),
        out_shape=[jax.ShapeDtypeStruct(t.shape, t.dtype) for t in tensors],
        in_specs=whole,
        out_specs=whole,
        scratch_shapes=[
            pltpu.SemaphoreType.DMA((count,)),
            pltpu.SemaphoreType.DMA((count,)),
            pltpu.SemaphoreType.DMA((count,)),
        ],
        compiler_params=pltpu.CompilerParams(
            collective_id=collective_id, has_side_effects=True, vmem_limit_bytes=32 << 20
        ),
    )(*tensors)


def to_patches(tensors, peers):
    def planes(t):
        clips, _, patches, width = t.shape
        t = t.reshape(clips, peers, patches // peers, width).transpose(1, 0, 2, 3)
        return t.reshape(peers, -1, width)

    clips, _, patches, width = tensors[0].shape
    arrived = exchange([planes(t) for t in tensors], 1)
    return [
        t.reshape(peers, clips, patches // peers, width).transpose(1, 0, 2, 3) for t in arrived
    ]


def to_frames(tensors, peers):
    clips, _, patches, width = tensors[0].shape
    arrived = exchange([t.transpose(1, 0, 2, 3).reshape(peers, -1, width) for t in tensors], 2)
    return [
        t.reshape(peers, clips, patches, width)
        .transpose(1, 0, 2, 3)
        .reshape(clips, 1, peers * patches, width)
        for t in arrived
    ]


def split_heads(tensor):
    return tensor.reshape(tensor.shape[:-1] + (HEADS, tensor.shape[-1] // HEADS))


def softmax_weights(queries, key_states):
    scaling = 1.0 / math.sqrt(queries.shape[-1] // HEADS)
    scores = (
        jnp.einsum(
            "cfxhd,cgxhd->cxhfg",
            split_heads(queries),
            split_heads(key_states),
            preferred_element_type=jnp.float32,
        )
        * scaling
    )
    return jax.nn.softmax(scores, axis=-1)


def attend(queries, key_states, value_states):
    weights = softmax_weights(queries, key_states).astype(jnp.bfloat16)
    heads_out = jnp.einsum(
        "cxhfg,cgxhd->cfxhd", weights, split_heads(value_states), preferred_element_type=jnp.float32
    )
    return heads_out.reshape(queries.shape).astype(jnp.bfloat16)


def attend_back(queries, key_states, value_states, attended_grad):
    scaling = 1.0 / math.sqrt(queries.shape[-1] // HEADS)
    probability = softmax_weights(queries, key_states)
    weights = probability.astype(jnp.bfloat16)
    grad_heads = split_heads(attended_grad)
    weight_grad = jnp.einsum(
        "cfxhd,cgxhd->cxhfg",
        grad_heads,
        split_heads(value_states),
        preferred_element_type=jnp.float32,
    )
    centred = weight_grad - jnp.sum(probability * weight_grad, axis=-1, keepdims=True)
    score_grad = (probability * centred * scaling).astype(jnp.bfloat16)
    query_grad = jnp.einsum(
        "cxhfg,cgxhd->cfxhd",
        score_grad,
        split_heads(key_states),
        preferred_element_type=jnp.float32,
    )
    key_grad = jnp.einsum(
        "cxhfg,cfxhd->cgxhd", score_grad, split_heads(queries), preferred_element_type=jnp.float32
    )
    value_grad = jnp.einsum(
        "cxhfg,cfxhd->cgxhd", weights, grad_heads, preferred_element_type=jnp.float32
    )
    return tuple(
        (
            tensor.reshape(queries.shape).astype(jnp.bfloat16)
            for tensor in (query_grad, key_grad, value_grad)
        )
    )


def body(queries, key_states, value_states, gate_vector, out_weight, cotangent):
    peers = lax.axis_size("seq")
    query_local, key_local, value_local = to_patches((queries, key_states, value_states), peers)
    attended = attend(query_local, key_local, value_local)
    row_count = attended.shape[0] * attended.shape[1] * attended.shape[2]
    feature_count = attended.shape[3]
    flat_attended = attended.reshape(row_count, feature_count)
    gate_wide = gate_vector[:, None, None, :]
    mixed_grad = (
        (gate_wide * cotangent.astype(jnp.float32))
        .astype(jnp.bfloat16)
        .reshape(row_count, feature_count)
    )
    projected = lax.dot_general(
        flat_attended,
        lax.all_gather(out_weight, "seq", axis=0, tiled=True),
        (((1,), (1,)), ((), ())),
        preferred_element_type=jnp.float32,
    )
    columns = mixed_grad
    attended_grad = jnp.dot(
        columns,
        lax.all_gather(out_weight, "seq", axis=0, tiled=True),
        preferred_element_type=jnp.float32,
    )
    branch = (gate_wide * projected.reshape(attended.shape)).astype(jnp.bfloat16)
    query_grad, key_grad, value_grad = attend_back(
        query_local,
        key_local,
        value_local,
        attended_grad.astype(jnp.bfloat16).reshape(attended.shape),
    )
    grad_query, grad_key, grad_value = to_frames((query_grad, key_grad, value_grad), peers)
    token_count = row_count * lax.axis_size("dp") * lax.axis_size("seq")
    inverse_root = 1.0 / math.sqrt(token_count)
    columns = mixed_grad
    seq_sum = lax.psum_scatter(
        (
            lax.dot_general(
                columns, flat_attended, (((0,), (0,)), ((), ())), preferred_element_type=jnp.float32
            )
            * inverse_root
        ).astype(jnp.bfloat16),
        "seq",
        scatter_dimension=0,
        tiled=True,
    ).astype(jnp.float32)
    grad_weight = lax.psum(seq_sum, "dp")
    return (branch, grad_query, grad_key, grad_value, grad_weight)


def solution(mesh):
    placed = (
        P("dp", "seq", None, None),
        P("dp", "seq", None, None),
        P("dp", "seq", None, None),
        P("dp", None),
        P("seq", None),
        P("dp", None, "seq", None),
    )
    return jax.shard_map(
        body,
        mesh=mesh,
        in_specs=placed,
        out_specs=(
            P("dp", None, "seq", None),
            P("dp", "seq", None, None),
            P("dp", "seq", None, None),
            P("dp", "seq", None, None),
            P("seq", None),
        ),
        check_vma=False,
    )
```

```python
import functools
import math

import jax
import jax.numpy as jnp
from jax import lax
from jax.experimental import pallas as pl
from jax.experimental.pallas import tpu as pltpu
from jax.sharding import PartitionSpec as P

HEADS = 16
MESH = pl.DeviceIdType.MESH
F32 = jnp.float32
BF16 = jnp.bfloat16
NT = (((1,), (1,)), ((), ()))
NN = (((1,), (0,)), ((), ()))
TN = (((0,), (0,)), ((), ()))


def dot(a, b, dims):
    return lax.dot_general(a, b, dims, preferred_element_type=F32)


def up8(n):
    return -(-n // 8) * 8


def kernel(
    n_y,
    n_z,
    tokens,
    q_in,
    k_in,
    v_in,
    dm_in,
    gate_in,
    w_in,
    branch_out,
    gq_out,
    gk_out,
    gv_out,
    gw_out,
    q_rec,
    k_rec,
    v_rec,
    q_rows,
    k_rows,
    v_rows,
    w_rec,
    w_full,
    bias,
    probs,
    d_att,
    wide,
    wide2,
    gq_send,
    gk_send,
    gv_send,
    dm_rows,
    dm_sib,
    att,
    att_sib,
    x_own,
    x_send,
    x_rec,
    x_sum,
    z_send,
    z_rec,
    y_rec,
    fin,
    a2a_send,
    a2a_recv,
    a2a_own,
    w_send,
    w_recv,
    sib_send,
    sib_recv,
    x_ssem,
    x_rsem,
    r_send,
    r_recv,
):
    peers, group, width = q_in.shape
    rows = peers * group
    head = width // HEADS
    scale = 1.0 / math.sqrt(head)
    own_rows = w_in.shape[0]
    half = own_rows // 2
    dp, seq = lax.axis_index("dp"), lax.axis_index("seq")
    y, x_hi = lax.div(dp, 2), lax.rem(dp, 2)
    core, z, x_lo = lax.rem(seq, 2), lax.rem(lax.div(seq, 2), n_z), lax.div(seq, 2 * n_z)
    x = 2 * x_hi + x_lo

    def at(y_=None, x_=None, z_=None, core_=None):
        y_ = y if y_ is None else y_
        x_ = x if x_ is None else x_
        z_ = z if z_ is None else z_
        core_ = core if core_ is None else core_
        return (2 * y_ + lax.div(x_, 2), (lax.rem(x_, 2) * n_z + z_) * 2 + core_)

    def remote(src, dst, send, recv, to):
        return pltpu.make_async_remote_copy(
            src_ref=src,
            dst_ref=dst,
            send_sem=send,
            recv_sem=recv,
            device_id=to,
            device_id_type=MESH,
        )

    sibling = at(core_=1 - core)
    ahead, behind = at(x_=lax.rem(x + 1, 4)), at(x_=lax.rem(x + 3, 4))

    barrier = pltpu.get_barrier_semaphore()

    def greet(to):
        pl.semaphore_signal(barrier, inc=1, device_id=to, device_id_type=MESH)

    def greet_seq(step, carry):
        greet((dp, lax.rem(seq + step, peers)))
        return carry

    lax.fori_loop(1, peers, greet_seq, 0)
    for step in range(1, n_y):
        greet(at(y_=lax.rem(y + step, n_y)))
    greet(at(x_=2 * (1 - x_hi)))
    greet(at(x_=2 * (1 - x_hi) + 1))
    pl.semaphore_wait(barrier, peers - 1 + n_y - 1 + 2)

    slot = lax.rem(z + y, n_z)
    w_first = remote(
        w_in,
        w_rec.at[core, x_lo, z],
        w_send.at[0],
        w_recv.at[0],
        at(z_=lax.rem(z - y + n_z, n_z)),
    )
    w_own = pltpu.make_async_copy(w_in, w_rec.at[core, x_lo, z], w_recv.at[5])

    @pl.when(y != 0)
    def _():
        w_first.start()

    @pl.when(y == 0)
    def _():
        w_own.start()

    def spread(t, src, dst):
        def send(step, carry):
            target = lax.rem(seq + step, peers)
            remote(
                src.at[target], dst.at[seq], a2a_send.at[t], a2a_recv.at[t], (dp, target)
            ).start()
            return carry

        lax.fori_loop(1, peers, send, 0)
        pltpu.make_async_copy(src.at[seq], dst.at[seq], a2a_own.at[t]).start()

    def arrive(t, src, dst):
        remote(
            src.at[pl.ds(0, peers - 1)],
            dst.at[pl.ds(0, peers - 1)],
            a2a_send.at[t],
            a2a_recv.at[t],
            sibling,
        ).wait_recv()
        pltpu.make_async_copy(src.at[seq], dst.at[seq], a2a_own.at[t]).wait()

    def sent(t, src, dst):
        remote(
            src.at[pl.ds(0, peers - 1)],
            dst.at[pl.ds(0, peers - 1)],
            a2a_send.at[t],
            a2a_recv.at[t],
            sibling,
        ).wait_send()

    spread(0, q_in, q_rec)
    spread(1, k_in, k_rec)
    spread(2, v_in, v_rec)

    block = n_z * half
    d_mixed = dm_in[...]
    row = lax.broadcasted_iota(jnp.int32, (block, 1), 0)
    turn = sum((row >= half * j).astype(jnp.int32) for j in range(1, n_z))
    row = row + turn * (2 * own_rows - half)
    lane = lax.broadcasted_iota(jnp.int32, (block, width), 1)
    for c in range(2):
        for b in range(4):
            first = (b % 2) * n_z * 2 * own_rows + c * own_rows + (b // 2) * half
            pick = (lane == row + first).astype(F32).astype(BF16)
            dm_rows[c, b] = dot(pick, d_mixed, NT).astype(BF16)
    dm_share = remote(
        dm_rows.at[1 - core], dm_sib, sib_send.at[0], sib_recv.at[0], sibling
    )
    dm_share.start()

    row_of = lax.broadcasted_iota(jnp.int32, (rows, rows), 0)
    col_of = lax.broadcasted_iota(jnp.int32, (rows, rows), 1)
    bias[...] = jnp.where(lax.rem(row_of, group) == lax.rem(col_of, group), 0.0, -1e30)

    @pl.when(y != 0)
    def _():
        w_first.wait()

    @pl.when(y == 0)
    def _():
        w_own.wait()

    w_second = [
        remote(
            w_rec.at[core, x_lo, slot],
            w_rec.at[core, x_lo, slot],
            w_send.at[1],
            w_recv.at[1],
            at(y_=lax.rem(y + step, n_y)),
        )
        for step in range(1, n_y)
    ]
    for copy in w_second:
        copy.start()
    z_half = n_z // 2
    low, high = pl.ds(0, z_half), pl.ds(z_half, n_z - z_half)
    mine = w_rec.at[core, x_lo]
    w_third = (
        remote(mine.at[low], mine.at[low], w_send.at[2], w_recv.at[2], ahead),
        remote(mine.at[high], mine.at[high], w_send.at[3], w_recv.at[3], behind),
    )
    w_fourth = remote(w_rec.at[core], w_rec.at[core], w_send.at[4], w_recv.at[4], sibling)

    def wait_second():
        whole = w_rec.at[core, x_lo, pl.ds(0, n_y - 1)]
        copy = remote(whole, whole, w_send.at[1], w_recv.at[1], sibling)
        copy.wait_send()
        copy.wait_recv()

    wait_second()
    for copy in w_third:
        copy.start()

    def to_rows(dst, src):
        dst[...] = src[...].astype(F32).reshape(rows, width).astype(BF16)

    def cut(ref, h):
        return ref[:, h * head : (h + 1) * head]

    def softmax(h):
        score = dot(cut(k_rows, h), cut(q_rows, h), NT) + bias[...]
        top = jnp.max(score, axis=0, keepdims=True)
        grown = jnp.exp((score - top) * scale)
        probs[h] = grown * (1.0 / jnp.sum(grown, axis=0, keepdims=True))

    arrive(0, q_in, q_rec)
    arrive(1, k_in, k_rec)
    to_rows(q_rows, q_rec)
    to_rows(k_rows, k_rec)
    for h in range(HEADS // 2):
        softmax(h)
    for copy in w_third:
        copy.wait()
    w_fourth.start()
    for h in range(HEADS // 2, HEADS):
        softmax(h)
    w_fourth.wait()

    quad = 4 * own_rows
    for b in range(peers // 4):
        parts = []
        for s in range(4 * b, 4 * b + 4):
            parts.append(w_rec[s % 2, s // (2 * n_z), (s // 2) % n_z].astype(F32))
        w_full[b * quad : (b + 1) * quad, :] = jnp.concatenate(parts, axis=0).astype(BF16)
    d_att[...] = dot(d_mixed, w_full[...], NN).astype(BF16)
    for h in range(HEADS):
        wide[:, h * head : (h + 1) * head] = dot(probs[h].astype(BF16), cut(d_att, h), NN)
    gv_send[...] = wide[...].reshape(peers, group, width).astype(BF16)
    spread(3, gv_send, gv_out)

    arrive(2, v_in, v_rec)
    to_rows(v_rows, v_rec)
    for h in range(HEADS):
        wide[:, h * head : (h + 1) * head] = dot(probs[h].astype(BF16), cut(v_rows, h), TN)
    att[...] = wide[...].astype(BF16)
    att_share = remote(att, att_sib, sib_send.at[1], sib_recv.at[1], sibling)
    att_share.start()

    dm_share.wait_recv()
    for b in range(4):
        x_own[b] = dot(dm_rows[core, b], att[...], NN)
    att_share.wait_recv()
    inverse_root = 1.0 / math.sqrt(tokens)
    for b in range(4):
        total = (x_own[b] + dot(dm_sib[b], att_sib[...], NN)) * inverse_root
        x_own[b] = total
        x_send[b] = total.astype(BF16)
    x_copies = []
    for step in (1, 3, 2):
        to = lax.rem(x + step, 4)
        x_copies.append(
            remote(
                x_send.at[to], x_rec.at[step], x_ssem.at[step], x_rsem.at[step], at(x_=to)
            )
        )
        x_copies[-1].start()

    mixed = dot(att[...], w_full[...], NT).reshape(peers, group, width)
    branch_out[...] = (mixed * gate_in[...][None]).reshape(rows, width).astype(BF16)

    for h in range(HEADS):
        prob = probs[h]
        d_prob = dot(cut(v_rows, h), cut(d_att, h), NT)
        centre = jnp.sum(prob * d_prob, axis=0, keepdims=True)
        d_score = (prob * (d_prob - centre) * scale).astype(BF16)
        wide[:, h * head : (h + 1) * head] = dot(d_score, cut(k_rows, h), TN)
        wide2[:, h * head : (h + 1) * head] = dot(d_score, cut(q_rows, h), NN)
    gq_send[...] = wide[...].reshape(peers, group, width).astype(BF16)
    spread(4, gq_send, gq_out)
    gk_send[...] = wide2[...].reshape(peers, group, width).astype(BF16)
    spread(5, gk_send, gk_out)

    for copy in x_copies:
        copy.wait()
    total = x_own[x]
    for step in range(1, 4):
        total += x_rec[step].astype(F32)
    x_sum[...] = total
    z_send[...] = jnp.zeros_like(z_send)
    for j in range(n_z):
        z_send[j, :half, :] = x_sum[j * half : (j + 1) * half, :].astype(BF16)
    for step in range(1, n_z):
        to = lax.rem(z + step, n_z)
        remote(z_send.at[to], z_rec.at[z], r_send.at[0], r_recv.at[0], at(z_=to)).start()
    z_rec[z] = z_send[z]
    z_all = remote(
        z_send.at[pl.ds(0, n_z - 1)],
        z_rec.at[pl.ds(0, n_z - 1)],
        r_send.at[0],
        r_recv.at[0],
        sibling,
    )
    z_all.wait_recv()

    total = z_rec[0].astype(F32)
    for j in range(1, n_z):
        total += z_rec[j].astype(F32)
    y_rec[y] = total.astype(BF16)
    for step in range(1, n_y):
        remote(
            y_rec.at[y],
            y_rec.at[y],
            r_send.at[1],
            r_recv.at[1],
            at(y_=lax.rem(y + step, n_y)),
        ).start()
    y_part = y_rec.at[pl.ds(0, n_y - 1)]
    y_all = remote(y_part, y_part, r_send.at[1], r_recv.at[1], sibling)
    y_all.wait_recv()
    total = y_rec[0].astype(F32)
    for j in range(1, n_y):
        total += y_rec[j].astype(F32)
    fin[x_hi] = total
    last = remote(
        fin.at[x_hi], fin.at[x_hi], r_send.at[2], r_recv.at[2], at(x_=lax.rem(x + 2, 4))
    )
    last.start()
    last.wait()
    gw_out[:half, :] = fin[0, :half, :]
    gw_out[half:, :] = fin[1, :half, :]

    arrive(3, gv_send, gv_out)
    arrive(4, gq_send, gq_out)
    arrive(5, gk_send, gk_out)
    sent(0, q_in, q_rec)
    sent(1, k_in, k_rec)
    sent(2, v_in, v_rec)
    sent(3, gv_send, gv_out)
    sent(4, gq_send, gq_out)
    sent(5, gk_send, gk_out)
    dm_share.wait_send()
    att_share.wait_send()
    z_all.wait_send()
    y_all.wait_send()


def body(n_y, n_z, tokens, queries, key_states, value_states, gate_vector, out_weight, cotangent):
    clips, frames, patches, width = cotangent.shape
    group, rows = clips * patches, clips * patches * frames
    own_rows = out_weight.shape[0]
    half = own_rows // 2
    block = n_z * half

    def planes(t):
        return (
            t.reshape(clips, frames, patches, width)
            .transpose(1, 0, 2, 3)
            .reshape(frames, group, width)
        )

    d_mixed = (
        (planes(cotangent).astype(F32).reshape(frames, clips, patches, width)
         * gate_vector[None, :, None, :])
        .astype(BF16)
        .reshape(rows, width)
    )
    gate_rows = jnp.repeat(gate_vector, patches, axis=0)
    plane = jax.ShapeDtypeStruct((frames, group, width), BF16)
    vmem = pl.BlockSpec(memory_space=pltpu.VMEM)
    flat = pltpu.VMEM((rows, width), BF16)
    flat32 = pltpu.VMEM((rows, width), F32)
    stack = pltpu.VMEM((frames, group, width), BF16)
    dma = pltpu.SemaphoreType.DMA
    branch, gq, gk, gv, gw = pl.pallas_call(
        functools.partial(kernel, n_y, n_z, tokens),
        out_shape=[
            jax.ShapeDtypeStruct((rows, width), BF16),
            plane,
            plane,
            plane,
            jax.ShapeDtypeStruct((own_rows, width), F32),
        ],
        in_specs=[vmem] * 6,
        out_specs=[vmem] * 5,
        scratch_shapes=[
            stack,
            stack,
            stack,
            flat,
            flat,
            flat,
            pltpu.VMEM((2, 2, n_z, own_rows, width), BF16),
            pltpu.VMEM((width, width), BF16),
            pltpu.VMEM((rows, rows), F32),
            pltpu.VMEM((HEADS, rows, rows), F32),
            flat,
            flat32,
            flat32,
            stack,
            stack,
            stack,
            pltpu.VMEM((2, 4, block, rows), BF16),
            pltpu.VMEM((4, block, rows), BF16),
            flat,
            flat,
            pltpu.VMEM((4, block, width), F32),
            pltpu.VMEM((4, block, width), BF16),
            pltpu.VMEM((4, block, width), BF16),
            pltpu.VMEM((block, width), F32),
            pltpu.VMEM((n_z, up8(half), width), BF16),
            pltpu.VMEM((n_z, up8(half), width), BF16),
            pltpu.VMEM((n_y, up8(half), width), BF16),
            pltpu.VMEM((2, up8(half), width), F32),
            dma((6,)),
            dma((6,)),
            dma((6,)),
            dma((5,)),
            dma((6,)),
            dma((2,)),
            dma((2,)),
            dma((4,)),
            dma((4,)),
            dma((3,)),
            dma((3,)),
        ],
        compiler_params=pltpu.CompilerParams(
            collective_id=1, has_side_effects=True, vmem_limit_bytes=56 << 20
        ),
    )(planes(queries), planes(key_states), planes(value_states), d_mixed, gate_rows, out_weight)

    def by_clip(t):
        return t.reshape(frames, clips, patches, width).transpose(1, 0, 2, 3)

    def home(t):
        return by_clip(t).reshape(queries.shape)

    return by_clip(branch), home(gq), home(gk), home(gv), gw


def solution(mesh):
    n_dp, n_seq = mesh.shape["dp"], mesh.shape["seq"]

    def step(queries, key_states, value_states, gate_vector, out_weight, cotangent):
        clips, frames, patches, _ = cotangent.shape
        tokens = clips * frames * patches * n_dp * n_seq
        return body(
            n_dp // 2,
            n_seq // 4,
            tokens,
            queries,
            key_states,
            value_states,
            gate_vector,
            out_weight,
            cotangent,
        )

    framed = P("dp", "seq", None, None)
    patched = P("dp", None, "seq", None)
    return jax.shard_map(
        step,
        mesh=mesh,
        in_specs=(framed, framed, framed, P("dp", None), P("seq", None), patched),
        out_specs=(patched, framed, framed, framed, P("seq", None)),
        check_vma=False,
    )
```

```python
import functools
import math

import jax
import jax.numpy as jnp
from jax import lax
from jax.experimental import pallas as pl
from jax.experimental.pallas import tpu as pltpu
from jax.sharding import PartitionSpec as P

HEADS = 16
MESH = pl.DeviceIdType.MESH
F32 = jnp.float32
BF16 = jnp.bfloat16
NT = (((1,), (1,)), ((), ()))
NN = (((1,), (0,)), ((), ()))
TN = (((0,), (0,)), ((), ()))


def dot(a, b, dims):
    return lax.dot_general(a, b, dims, preferred_element_type=F32)


def up8(n):
    return -(-n // 8) * 8


def kernel(
    n_y,
    n_z,
    tokens,
    q_in,
    k_in,
    v_in,
    cot_in,
    gate_in,
    w_in,
    branch_out,
    gq_out,
    gk_out,
    gv_out,
    gw_out,
    q_pl,
    k_pl,
    v_pl,
    d_mix,
    q_rec,
    k_rec,
    v_rec,
    q_rows,
    k_rows,
    v_rows,
    w_rec,
    w_full,
    bias,
    probs,
    d_att,
    wide,
    wide2,
    gq_send,
    gk_send,
    gv_send,
    dm_rows,
    dm_sib,
    att,
    att_sib,
    x_own,
    x_send,
    x_rec,
    x_sum,
    z_send,
    z_rec,
    y_rec,
    fin,
    a2a_send,
    a2a_recv,
    a2a_own,
    w_send,
    w_recv,
    wy_recv,
    wx_recv,
    sib_send,
    sib_recv,
    x_ssem,
    x_rsem,
    r_send,
    r_recv,
):
    peers, group, width = q_rec.shape
    rows = peers * group
    head = width // HEADS
    scale = 1.0 / math.sqrt(head)
    own_rows = w_in.shape[0]
    half = own_rows // 2
    dp, seq = lax.axis_index("dp"), lax.axis_index("seq")
    y, x_hi = lax.div(dp, 2), lax.rem(dp, 2)
    core, z, x_lo = lax.rem(seq, 2), lax.rem(lax.div(seq, 2), n_z), lax.div(seq, 2 * n_z)
    x = 2 * x_hi + x_lo

    def at(y_=None, x_=None, z_=None, core_=None):
        y_ = y if y_ is None else y_
        x_ = x if x_ is None else x_
        z_ = z if z_ is None else z_
        core_ = core if core_ is None else core_
        return (2 * y_ + lax.div(x_, 2), (lax.rem(x_, 2) * n_z + z_) * 2 + core_)

    def remote(src, dst, send, recv, to):
        return pltpu.make_async_remote_copy(
            src_ref=src,
            dst_ref=dst,
            send_sem=send,
            recv_sem=recv,
            device_id=to,
            device_id_type=MESH,
        )

    sibling = at(core_=1 - core)
    ahead, behind = at(x_=lax.rem(x + 1, 4)), at(x_=lax.rem(x + 3, 4))

    barrier = pltpu.get_barrier_semaphore()

    def greet(to):
        pl.semaphore_signal(barrier, inc=1, device_id=to, device_id_type=MESH)

    def greet_seq(step, carry):
        greet((dp, lax.rem(seq + step, peers)))
        return carry

    lax.fori_loop(1, peers, greet_seq, 0)
    for step in range(1, n_y):
        greet(at(y_=lax.rem(y + step, n_y)))
    greet(at(x_=2 * (1 - x_hi)))
    greet(at(x_=2 * (1 - x_hi) + 1))
    pl.semaphore_wait(barrier, peers - 1 + n_y - 1 + 2)

    slot = lax.rem(z + y, n_z)
    w_first = remote(
        w_in,
        w_rec.at[core, x_lo, z],
        w_send.at[0],
        w_recv.at[0],
        at(z_=lax.rem(z - y + n_z, n_z)),
    )
    w_own = pltpu.make_async_copy(w_in, w_rec.at[core, x_lo, z], w_recv.at[2])

    @pl.when(y != 0)
    def _():
        w_first.start()

    @pl.when(y == 0)
    def _():
        w_own.start()

    def spread(t, src, dst, first=1, last=None):
        def send(step, carry):
            target = lax.rem(seq + step, peers)
            remote(
                src.at[target], dst.at[seq], a2a_send.at[t], a2a_recv.at[t], (dp, target)
            ).start()
            return carry

        lax.fori_loop(first, last or peers, send, 0)
        if first == 1:
            pltpu.make_async_copy(src.at[seq], dst.at[seq], a2a_own.at[t]).start()

    def arrive(t, src, dst):
        remote(
            src.at[pl.ds(0, peers - 1)],
            dst.at[pl.ds(0, peers - 1)],
            a2a_send.at[t],
            a2a_recv.at[t],
            sibling,
        ).wait_recv()
        pltpu.make_async_copy(src.at[seq], dst.at[seq], a2a_own.at[t]).wait()

    def sent(t, src, dst):
        remote(
            src.at[pl.ds(0, peers - 1)],
            dst.at[pl.ds(0, peers - 1)],
            a2a_send.at[t],
            a2a_recv.at[t],
            sibling,
        ).wait_send()

    def deal(src, dst):
        first = src[0, 0].astype(F32).reshape(peers // 2, group, width)
        second = src[1, 0].astype(F32).reshape(peers // 2, group, width)
        each = group // 2
        even = jnp.concatenate([first[:, :each], second[:, :each]], axis=1)
        odd = jnp.concatenate([first[:, each:], second[:, each:]], axis=1)
        both = jnp.stack([even, odd], axis=1).reshape(peers, group, width)
        dst[...] = both.astype(BF16)

    deal(q_in, q_pl)
    spread(0, q_pl, q_rec)
    deal(k_in, k_pl)
    spread(1, k_pl, k_rec)
    deal(v_in, v_pl)
    spread(2, v_pl, v_rec)

    gate = jnp.concatenate(
        [jnp.broadcast_to(gate_in[c : c + 1, :], (group // 2, width)) for c in range(2)], axis=0
    )
    cot = jnp.concatenate([cot_in[0].astype(F32), cot_in[1].astype(F32)], axis=1)
    d_mix[...] = (cot * gate[None]).reshape(rows, width).astype(BF16)

    block = n_z * half
    d_mixed = d_mix[...]
    row = lax.broadcasted_iota(jnp.int32, (block, 1), 0)
    turn = sum((row >= half * j).astype(jnp.int32) for j in range(1, n_z))
    row = row + turn * (2 * own_rows - half)
    lane = lax.broadcasted_iota(jnp.int32, (block, width), 1)
    for c in range(2):
        for b in range(4):
            first = (b % 2) * n_z * 2 * own_rows + c * own_rows + (b // 2) * half
            pick = (lane == row + first).astype(F32).astype(BF16)
            dm_rows[c, b] = dot(pick, d_mixed, NT).astype(BF16)
    dm_share = remote(
        dm_rows.at[1 - core], dm_sib, sib_send.at[0], sib_recv.at[0], sibling
    )
    dm_share.start()

    row_of = lax.broadcasted_iota(jnp.int32, (rows, rows), 0)
    col_of = lax.broadcasted_iota(jnp.int32, (rows, rows), 1)
    bias[...] = jnp.where(lax.rem(row_of, group) == lax.rem(col_of, group), 0.0, -1e30)

    @pl.when(y != 0)
    def _():
        w_first.wait()

    @pl.when(y == 0)
    def _():
        w_own.wait()

    order = [1, 7, 2, 6, 3, 5, 4][:n_y - 1] if n_y == 8 else list(range(1, n_y))

    def shard(step, x_lo_):
        return w_rec.at[core, x_lo_, lax.rem(z + y - step + n_z, n_z)]

    def hop(step, x_lo_, send, recv, to):
        return remote(shard(step, x_lo_), shard(step, x_lo_), send, recv, to)

    def along_y(step):
        return hop(step, x_lo, w_send.at[1], wy_recv.at[step], sibling)

    def along_x(step, turn, x_lo_):
        to = ahead if turn % 2 else behind
        return hop(step, x_lo_, w_send.at[2], wx_recv.at[step], to)

    def across(step, x_lo_):
        return hop(step, x_lo_, w_send.at[3], w_recv.at[1], sibling)

    for step in order:
        remote(
            shard(0, x_lo),
            shard(0, x_lo),
            w_send.at[1],
            wy_recv.at[step],
            at(y_=lax.rem(y + step, n_y)),
        ).start()
    for turn, step in enumerate([0] + order):
        if step:
            along_y(step).wait_recv()
        along_x(step, turn, x_lo).start()
        across(step, x_lo).start()
    for turn, step in enumerate([0] + order):
        along_x(step, turn, 1 - x_lo).wait_recv()
        across(step, 1 - x_lo).start()

    def to_rows(dst, src):
        dst[...] = src[...].astype(F32).reshape(rows, width).astype(BF16)

    def cut(ref, h):
        return ref[:, h * head : (h + 1) * head]

    def softmax(h):
        score = dot(cut(k_rows, h), cut(q_rows, h), NT) + bias[...]
        top = jnp.max(score, axis=0, keepdims=True)
        grown = jnp.exp((score - top) * scale)
        probs[h] = grown * (1.0 / jnp.sum(grown, axis=0, keepdims=True))

    arrive(0, q_pl, q_rec)
    arrive(1, k_pl, k_rec)
    to_rows(q_rows, q_rec)
    to_rows(k_rows, k_rec)
    for h in range(HEADS):
        softmax(h)
    remote(
        w_rec.at[core], w_rec.at[1 - core], w_send.at[3], w_recv.at[1], sibling
    ).wait_recv()

    quad = 4 * own_rows
    for b in range(peers // 4):
        parts = []
        for s in range(4 * b, 4 * b + 4):
            parts.append(w_rec[s % 2, s // (2 * n_z), (s // 2) % n_z].astype(F32))
        w_full[b * quad : (b + 1) * quad, :] = jnp.concatenate(parts, axis=0).astype(BF16)
    d_att[...] = dot(d_mix[...], w_full[...], NN).astype(BF16)
    for h in range(HEADS):
        wide[:, h * head : (h + 1) * head] = dot(probs[h].astype(BF16), cut(d_att, h), NN)
    gv_send[...] = wide[...].reshape(peers, group, width).astype(BF16)
    spread(3, gv_send, gv_out)

    arrive(2, v_pl, v_rec)
    to_rows(v_rows, v_rec)
    for h in range(HEADS):
        wide[:, h * head : (h + 1) * head] = dot(probs[h].astype(BF16), cut(v_rows, h), TN)
    att[...] = wide[...].astype(BF16)
    att_share = remote(att, att_sib, sib_send.at[1], sib_recv.at[1], sibling)
    att_share.start()

    dm_share.wait_recv()
    for b in range(4):
        x_own[b] = dot(dm_rows[core, b], att[...], NN)
    att_share.wait_recv()
    inverse_root = 1.0 / math.sqrt(tokens)
    for b in range(4):
        total = (x_own[b] + dot(dm_sib[b], att_sib[...], NN)) * inverse_root
        x_own[b] = total
        x_send[b] = total.astype(BF16)
    x_copies = []
    for step in (1, 3, 2):
        to = lax.rem(x + step, 4)
        x_copies.append(
            remote(
                x_send.at[to], x_rec.at[step], x_ssem.at[step], x_rsem.at[step], at(x_=to)
            )
        )
        x_copies[-1].start()

    mixed = dot(att[...], w_full[...], NT).reshape(peers, group, width)
    mixed = (mixed * gate[None]).astype(BF16)
    for c in range(2):
        branch_out[c] = mixed[:, c * (group // 2) : (c + 1) * (group // 2), :]

    for h in range(HEADS):
        prob = probs[h]
        d_prob = dot(cut(v_rows, h), cut(d_att, h), NT)
        centre = jnp.sum(prob * d_prob, axis=0, keepdims=True)
        d_score = (prob * (d_prob - centre) * scale).astype(BF16)
        wide[:, h * head : (h + 1) * head] = dot(d_score, cut(k_rows, h), TN)
        wide2[:, h * head : (h + 1) * head] = dot(d_score, cut(q_rows, h), NN)
    gq_send[...] = wide[...].reshape(peers, group, width).astype(BF16)
    spread(4, gq_send, gq_out)
    gk_send[...] = wide2[...].reshape(peers, group, width).astype(BF16)
    spread(5, gk_send, gk_out, 1, peers // 2)

    for copy in x_copies:
        copy.wait()
    total = x_own[x]
    for step in range(1, 4):
        total += x_rec[step].astype(F32)
    x_sum[...] = total
    z_send[...] = jnp.zeros_like(z_send)
    for j in range(n_z):
        z_send[j, :half, :] = x_sum[j * half : (j + 1) * half, :].astype(BF16)
    for step in range(1, n_z):
        to = lax.rem(z + step, n_z)
        remote(z_send.at[to], z_rec.at[z], r_send.at[0], r_recv.at[0], at(z_=to)).start()
    spread(5, gk_send, gk_out, peers // 2, peers)
    z_rec[z] = z_send[z]
    z_all = remote(
        z_send.at[pl.ds(0, n_z - 1)],
        z_rec.at[pl.ds(0, n_z - 1)],
        r_send.at[0],
        r_recv.at[0],
        sibling,
    )
    z_all.wait_recv()

    total = z_rec[0].astype(F32)
    for j in range(1, n_z):
        total += z_rec[j].astype(F32)
    y_rec[y] = total.astype(BF16)
    for step in range(1, n_y):
        remote(
            y_rec.at[y],
            y_rec.at[y],
            r_send.at[1],
            r_recv.at[1],
            at(y_=lax.rem(y + step, n_y)),
        ).start()
    y_part = y_rec.at[pl.ds(0, n_y - 1)]
    y_all = remote(y_part, y_part, r_send.at[1], r_recv.at[1], sibling)
    y_all.wait_recv()
    total = y_rec[0].astype(F32)
    for j in range(1, n_y):
        total += y_rec[j].astype(F32)
    fin[x_hi] = total
    last = remote(
        fin.at[x_hi], fin.at[x_hi], r_send.at[2], r_recv.at[2], at(x_=lax.rem(x + 2, 4))
    )
    last.start()
    last.wait()
    gw_out[:half, :] = fin[0, :half, :]
    gw_out[half:, :] = fin[1, :half, :]

    arrive(3, gv_send, gv_out)
    arrive(4, gq_send, gq_out)
    arrive(5, gk_send, gk_out)
    sent(0, q_pl, q_rec)
    sent(1, k_pl, k_rec)
    sent(2, v_pl, v_rec)
    sent(3, gv_send, gv_out)
    sent(4, gq_send, gq_out)
    sent(5, gk_send, gk_out)
    row_sent = w_rec.at[core, x_lo, pl.ds(0, n_y - 1)]
    remote(row_sent, row_sent, w_send.at[1], w_recv.at[1], sibling).wait_send()
    all_sent = w_rec.at[core, x_lo]
    remote(all_sent, all_sent, w_send.at[2], w_recv.at[1], sibling).wait_send()
    remote(w_rec.at[core], w_rec.at[core], w_send.at[3], w_recv.at[1], sibling).wait_send()
    dm_share.wait_send()
    att_share.wait_send()
    z_all.wait_send()
    y_all.wait_send()


def settle(
    branch_in,
    gq_in,
    gk_in,
    gv_in,
    gw_in,
    branch_out,
    gq_out,
    gk_out,
    gv_out,
    gw_out,
    gq_pl,
    gk_pl,
    gv_pl,
    gq_own,
    gk_own,
    gv_own,
    branch_own,
    gw_own,
    sem,
):
    copies = [
        pltpu.make_async_copy(src, dst, sem.at[i])
        for i, (src, dst) in enumerate(
            (
                (gv_in, gv_pl),
                (gq_in, gq_pl),
                (gk_in, gk_pl),
                (branch_in, branch_own),
                (gw_in, gw_own),
            )
        )
    ]
    for copy in copies:
        copy.start()
    triples = ((gv_pl, gv_own, gv_out), (gq_pl, gq_own, gq_out), (gk_pl, gk_own, gk_out))
    for i, (src, own, dst) in enumerate(triples):
        peers, group, width = src.shape
        each = group // 2
        copies[i].wait()
        pairs = src[...].astype(F32).reshape(peers // 2, 2, group, width)
        even, odd = pairs[:, 0], pairs[:, 1]
        for c in range(2):
            part = slice(c * each, (c + 1) * each)
            both = jnp.concatenate([even[:, part], odd[:, part]], axis=1)
            own[c, 0] = both.reshape(peers * each, width).astype(BF16)
        copies.append(pltpu.make_async_copy(own, dst, sem.at[5 + i]))
        copies[-1].start()
    for i, (own, dst) in ((3, (branch_own, branch_out)), (4, (gw_own, gw_out))):
        copies[i].wait()
        copies.append(pltpu.make_async_copy(own, dst, sem.at[5 + i]))
        copies[-1].start()
    for copy in copies[5:]:
        copy.wait()


def body(n_y, n_z, tokens, queries, key_states, value_states, gate_vector, out_weight, cotangent):
    clips, frames, patches, width = cotangent.shape
    group, rows = clips * patches, clips * patches * frames
    own_rows = out_weight.shape[0]
    half = own_rows // 2
    block = n_z * half

    plane = jax.ShapeDtypeStruct((frames, group, width), BF16)
    vmem = pl.BlockSpec(memory_space=pltpu.VMEM)
    flat = pltpu.VMEM((rows, width), BF16)
    flat32 = pltpu.VMEM((rows, width), F32)
    stack = pltpu.VMEM((frames, group, width), BF16)
    dma = pltpu.SemaphoreType.DMA
    branch, gq, gk, gv, gw = pl.pallas_call(
        functools.partial(kernel, n_y, n_z, tokens),
        out_shape=[
            jax.ShapeDtypeStruct(cotangent.shape, BF16),
            plane,
            plane,
            plane,
            jax.ShapeDtypeStruct((own_rows, width), F32),
        ],
        in_specs=[vmem] * 6,
        out_specs=[vmem] * 5,
        scratch_shapes=[
            stack,
            stack,
            stack,
            flat,
            stack,
            stack,
            stack,
            flat,
            flat,
            flat,
            pltpu.VMEM((2, 2, n_z, own_rows, width), BF16),
            pltpu.VMEM((width, width), BF16),
            pltpu.VMEM((rows, rows), F32),
            pltpu.VMEM((HEADS, rows, rows), F32),
            flat,
            flat32,
            flat32,
            stack,
            stack,
            stack,
            pltpu.VMEM((2, 4, block, rows), BF16),
            pltpu.VMEM((4, block, rows), BF16),
            flat,
            flat,
            pltpu.VMEM((4, block, width), F32),
            pltpu.VMEM((4, block, width), BF16),
            pltpu.VMEM((4, block, width), BF16),
            pltpu.VMEM((block, width), F32),
            pltpu.VMEM((n_z, up8(half), width), BF16),
            pltpu.VMEM((n_z, up8(half), width), BF16),
            pltpu.VMEM((n_y, up8(half), width), BF16),
            pltpu.VMEM((2, up8(half), width), F32),
            dma((6,)),
            dma((6,)),
            dma((6,)),
            dma((4,)),
            dma((3,)),
            dma((n_y,)),
            dma((n_y,)),
            dma((2,)),
            dma((2,)),
            dma((4,)),
            dma((4,)),
            dma((3,)),
            dma((3,)),
        ],
        compiler_params=pltpu.CompilerParams(
            collective_id=1, has_side_effects=True, vmem_limit_bytes=56 << 20
        ),
    )(queries, key_states, value_states, cotangent, gate_vector, out_weight)

    whole = pl.BlockSpec(memory_space=pltpu.HBM)
    own = pltpu.VMEM(queries.shape, BF16)
    return pl.pallas_call(
        settle,
        out_shape=[
            jax.ShapeDtypeStruct(branch.shape, branch.dtype),
            jax.ShapeDtypeStruct(queries.shape, BF16),
            jax.ShapeDtypeStruct(queries.shape, BF16),
            jax.ShapeDtypeStruct(queries.shape, BF16),
            jax.ShapeDtypeStruct(gw.shape, gw.dtype),
        ],
        in_specs=[whole] * 5,
        out_specs=[whole] * 5,
        scratch_shapes=[
            stack,
            stack,
            stack,
            own,
            own,
            own,
            pltpu.VMEM(branch.shape, branch.dtype),
            pltpu.VMEM(gw.shape, gw.dtype),
            dma((10,)),
        ],
        compiler_params=pltpu.CompilerParams(vmem_limit_bytes=60 << 20),
    )(branch, gq, gk, gv, gw)


def solution(mesh):
    n_dp, n_seq = mesh.shape["dp"], mesh.shape["seq"]

    def step(queries, key_states, value_states, gate_vector, out_weight, cotangent):
        clips, frames, patches, _ = cotangent.shape
        tokens = clips * frames * patches * n_dp * n_seq
        return body(
            n_dp // 2,
            n_seq // 4,
            tokens,
            queries,
            key_states,
            value_states,
            gate_vector,
            out_weight,
            cotangent,
        )

    framed = P("dp", "seq", None, None)
    patched = P("dp", None, "seq", None)
    return jax.shard_map(
        step,
        mesh=mesh,
        in_specs=(framed, framed, framed, P("dp", None), P("seq", None), patched),
        out_specs=(patched, framed, framed, framed, P("seq", None)),
        check_vma=False,
    )
```

```python
import functools
import math

import jax
import jax.numpy as jnp
from jax import lax
from jax.experimental import pallas as pl
from jax.experimental.pallas import tpu as pltpu
from jax.sharding import PartitionSpec as P

HEADS = 16
MESH = pl.DeviceIdType.MESH
F32 = jnp.float32
BF16 = jnp.bfloat16
NT = (((1,), (1,)), ((), ()))
NN = (((1,), (0,)), ((), ()))
TN = (((0,), (0,)), ((), ()))


def dot(a, b, dims):
    return lax.dot_general(a, b, dims, preferred_element_type=F32)


def up8(n):
    return -(-n // 8) * 8


def kernel(
    n_y,
    n_z,
    tokens,
    q_in,
    k_in,
    v_in,
    cot_in,
    gate_in,
    w_in,
    branch_out,
    gq_out,
    gk_out,
    gv_out,
    gw_out,
    q_pl,
    k_pl,
    v_pl,
    d_mix,
    q_rec,
    k_rec,
    v_rec,
    q_rows,
    k_rows,
    v_rows,
    w_rec,
    w_full,
    bias,
    probs,
    d_att,
    wide,
    wide2,
    gq_send,
    gk_send,
    gv_send,
    dm_rows,
    dm_sib,
    p_turn,
    att_l,
    att_r,
    att_l_sib,
    att_r_sib,
    dn_rows,
    dn_sib,
    a_own,
    a_send,
    a_rec,
    a_part,
    a_got,
    b_own,
    b_send,
    b_rec,
    b_part,
    b_got,
    c_send,
    c_rec,
    fin,
    a2a_send,
    a2a_recv,
    a2a_own,
    w_send,
    w_recv,
    wy_recv,
    wx_recv,
    sib_send,
    sib_recv,
    a_ssem,
    a_rsem,
    r_send,
    r_recv,
    fin_recv,
):
    peers, group, width = q_rec.shape
    rows = peers * group
    head = width // HEADS
    scale = 1.0 / math.sqrt(head)
    own_rows = w_in.shape[0]
    half = own_rows // 2
    dp, seq = lax.axis_index("dp"), lax.axis_index("seq")
    y, x_hi = lax.div(dp, 2), lax.rem(dp, 2)
    core, z, x_lo = lax.rem(seq, 2), lax.rem(lax.div(seq, 2), n_z), lax.div(seq, 2 * n_z)
    x = 2 * x_hi + x_lo

    def at(y_=None, x_=None, z_=None, core_=None):
        y_ = y if y_ is None else y_
        x_ = x if x_ is None else x_
        z_ = z if z_ is None else z_
        core_ = core if core_ is None else core_
        return (2 * y_ + lax.div(x_, 2), (lax.rem(x_, 2) * n_z + z_) * 2 + core_)

    def remote(src, dst, send, recv, to):
        return pltpu.make_async_remote_copy(
            src_ref=src,
            dst_ref=dst,
            send_sem=send,
            recv_sem=recv,
            device_id=to,
            device_id_type=MESH,
        )

    sibling = at(core_=1 - core)
    ahead, behind = at(x_=lax.rem(x + 1, 4)), at(x_=lax.rem(x + 3, 4))

    barrier = pltpu.get_barrier_semaphore()

    def greet(to):
        pl.semaphore_signal(barrier, inc=1, device_id=to, device_id_type=MESH)

    def greet_seq(step, carry):
        greet((dp, lax.rem(seq + step, peers)))
        return carry

    lax.fori_loop(1, peers, greet_seq, 0)
    n_dp = 2 * n_y

    def greet_dp(step, carry):
        greet((lax.rem(dp + step, n_dp), seq))
        return carry

    lax.fori_loop(1, n_dp, greet_dp, 0)
    greet(at(x_=2 * (1 - x_hi) + 1 - x_lo))
    pl.semaphore_wait(barrier, peers + n_dp - 1)

    slot = lax.rem(z + y, n_z)
    w_first = remote(
        w_in,
        w_rec.at[core, x_lo, z],
        w_send.at[0],
        w_recv.at[0],
        at(z_=lax.rem(z - y + n_z, n_z)),
    )
    w_own = pltpu.make_async_copy(w_in, w_rec.at[core, x_lo, z], w_recv.at[2])

    @pl.when(y != 0)
    def _():
        w_first.start()

    @pl.when(y == 0)
    def _():
        w_own.start()

    def spread(t, src, dst, first=1, last=None):
        def send(step, carry):
            target = lax.rem(seq + step, peers)
            remote(
                src.at[target], dst.at[seq], a2a_send.at[t], a2a_recv.at[t], (dp, target)
            ).start()
            return carry

        lax.fori_loop(first, last or peers, send, 0)
        if first == 1:
            pltpu.make_async_copy(src.at[seq], dst.at[seq], a2a_own.at[t]).start()

    def arrive(t, src, dst):
        remote(
            src.at[pl.ds(0, peers - 1)],
            dst.at[pl.ds(0, peers - 1)],
            a2a_send.at[t],
            a2a_recv.at[t],
            sibling,
        ).wait_recv()
        pltpu.make_async_copy(src.at[seq], dst.at[seq], a2a_own.at[t]).wait()

    def sent(t, src, dst):
        remote(
            src.at[pl.ds(0, peers - 1)],
            dst.at[pl.ds(0, peers - 1)],
            a2a_send.at[t],
            a2a_recv.at[t],
            sibling,
        ).wait_send()

    def deal(src, dst):
        first = src[0, 0].astype(F32).reshape(peers // 2, group, width)
        second = src[1, 0].astype(F32).reshape(peers // 2, group, width)
        each = group // 2
        even = jnp.concatenate([first[:, :each], second[:, :each]], axis=1)
        odd = jnp.concatenate([first[:, each:], second[:, each:]], axis=1)
        both = jnp.stack([even, odd], axis=1).reshape(peers, group, width)
        dst[...] = both.astype(BF16)

    deal(q_in, q_pl)
    spread(0, q_pl, q_rec)
    deal(k_in, k_pl)
    spread(1, k_pl, k_rec)
    deal(v_in, v_pl)
    spread(2, v_pl, v_rec)

    @pl.when(y != 0)
    def _():
        w_first.wait()

    @pl.when(y == 0)
    def _():
        w_own.wait()

    order = [1, 7, 2, 6, 3, 5, 4][:n_y - 1] if n_y == 8 else list(range(1, n_y))

    def shard(step, x_lo_):
        return w_rec.at[core, x_lo_, lax.rem(z + y - step + n_z, n_z)]

    def hop(step, x_lo_, send, recv, to):
        return remote(shard(step, x_lo_), shard(step, x_lo_), send, recv, to)

    def along_y(step):
        return hop(step, x_lo, w_send.at[1], wy_recv.at[step], sibling)

    def along_x(step, turn, x_lo_):
        to = ahead if turn % 2 else behind
        return hop(step, x_lo_, w_send.at[2], wx_recv.at[step], to)

    def across(step, x_lo_):
        return hop(step, x_lo_, w_send.at[3], w_recv.at[1], sibling)

    for step in order:
        remote(
            shard(0, x_lo),
            shard(0, x_lo),
            w_send.at[1],
            wy_recv.at[step],
            at(y_=lax.rem(y + step, n_y)),
        ).start()
    along_x(0, 0, x_lo).start()
    across(0, x_lo).start()

    gate = jnp.concatenate(
        [jnp.broadcast_to(gate_in[c : c + 1, :], (group // 2, width)) for c in range(2)], axis=0
    )
    cot = jnp.concatenate([cot_in[0].astype(F32), cot_in[1].astype(F32)], axis=1)
    d_mix[...] = (cot * gate[None]).reshape(rows, width).astype(BF16)
    block, tall = n_z * half, 4 * half
    far = n_z * 2 * own_rows

    def picked(row, first):
        lane = lax.broadcasted_iota(jnp.int32, (row.shape[0], width), 1)
        pick = (lane == row + first).astype(F32).astype(BF16)
        return dot(pick, d_mix[...], NT).astype(BF16)

    def by_x(c):
        row = lax.broadcasted_iota(jnp.int32, (block, 1), 0)
        turn = sum((row >= half * j).astype(jnp.int32) for j in range(1, n_z))
        row = row + turn * (2 * own_rows - half)
        for b in range(4):
            dm_rows[c, b] = picked(row, (b % 2) * far + c * own_rows + (b // 2) * half)

    def by_z(c):
        row = lax.broadcasted_iota(jnp.int32, (tall, 1), 0)
        turn = sum((row >= half * j).astype(jnp.int32) for j in range(1, 4))
        upper = (row >= half * 2).astype(jnp.int32)
        row = row - turn * half + upper * half + (turn - 2 * upper) * far
        for j in range(n_z):
            dn_rows[c, j] = picked(row, j * 2 * own_rows + c * own_rows)

    def clear():
        row_of = lax.broadcasted_iota(jnp.int32, (rows, rows), 0)
        col_of = lax.broadcasted_iota(jnp.int32, (rows, rows), 1)
        bias[...] = jnp.where(lax.rem(row_of, group) == lax.rem(col_of, group), 0.0, -1e30)
        a_part[...] = jnp.zeros_like(a_part)
        b_part[...] = jnp.zeros_like(b_part)

    dm_share = remote(
        dm_rows.at[1 - core], dm_sib, sib_send.at[0], sib_recv.at[0], sibling
    )
    dn_share = remote(
        dn_rows.at[1 - core], dn_sib, sib_send.at[2], sib_recv.at[2], sibling
    )
    chores = [
        lambda: by_x(0),
        lambda: by_x(1),
        dm_share.start,
        lambda: by_z(0),
        lambda: by_z(1),
        dn_share.start,
        clear,
    ]
    for turn, step in enumerate(order, 1):
        along_y(step).wait_recv()
        along_x(step, turn, x_lo).start()
        across(step, x_lo).start()
        if chores:
            chores.pop(0)()
    for chore in chores:
        chore()
    for turn, step in enumerate([0] + order):
        along_x(step, turn, 1 - x_lo).wait_recv()
        across(step, 1 - x_lo).start()

    def to_rows(dst, src):
        dst[...] = src[...].astype(F32).reshape(rows, width).astype(BF16)

    def cut(ref, h):
        return ref[:, h * head : (h + 1) * head]

    def softmax(h):
        score = dot(cut(k_rows, h), cut(q_rows, h), NT) + bias[...]
        top = jnp.max(score, axis=0, keepdims=True)
        grown = jnp.exp((score - top) * scale)
        probs[h] = grown * (1.0 / jnp.sum(grown, axis=0, keepdims=True))

    arrive(0, q_pl, q_rec)
    arrive(1, k_pl, k_rec)
    to_rows(q_rows, q_rec)
    to_rows(k_rows, k_rec)
    for h in range(HEADS):
        softmax(h)
    remote(
        w_rec.at[core], w_rec.at[1 - core], w_send.at[3], w_recv.at[1], sibling
    ).wait_recv()

    quad = 4 * own_rows
    for b in range(peers // 4):
        parts = []
        for s in range(4 * b, 4 * b + 4):
            parts.append(w_rec[s % 2, s // (2 * n_z), (s // 2) % n_z].astype(F32))
        w_full[b * quad : (b + 1) * quad, :] = jnp.concatenate(parts, axis=0).astype(BF16)
    d_att[...] = dot(d_mix[...], w_full[...], NN).astype(BF16)
    for h in range(HEADS):
        wide[:, h * head : (h + 1) * head] = dot(probs[h].astype(BF16), cut(d_att, h), NN)
    gv_send[...] = wide[...].reshape(peers, group, width).astype(BF16)
    spread(3, gv_send, gv_out)

    for h in range(HEADS):
        p_turn[h] = probs[h].T.astype(BF16)

    cols = (width // 128 + 1) // 2 * 128
    left_heads = -(-cols // head)
    att_shares = (
        remote(att_l, att_l_sib, sib_send.at[1], sib_recv.at[1], sibling),
        remote(att_r, att_r_sib, sib_send.at[3], sib_recv.at[3], sibling),
    )
    arrive(2, v_pl, v_rec)
    to_rows(v_rows, v_rec)
    for h in range(left_heads):
        wide[:, h * head : (h + 1) * head] = dot(p_turn[h], cut(v_rows, h), NN)
    att_l[...] = wide[:, :cols].astype(BF16)
    att_shares[0].start()
    for h in range(left_heads, HEADS):
        wide[:, h * head : (h + 1) * head] = dot(p_turn[h], cut(v_rows, h), NN)
    att_r[...] = wide[:, cols:].astype(BF16)
    att_shares[1].start()

    def scored(h):
        prob = probs[h]
        d_prob = dot(cut(v_rows, h), cut(d_att, h), NT)
        centre = jnp.sum(prob * d_prob, axis=0, keepdims=True)
        d_score = (prob * (d_prob - centre) * scale).astype(BF16)
        wide[:, h * head : (h + 1) * head] = dot(d_score, cut(k_rows, h), TN)
        wide2[:, h * head : (h + 1) * head] = dot(d_score, cut(q_rows, h), NN)

    ahead_heads = HEADS // 4
    for h in range(ahead_heads):
        scored(h)

    dm_share.wait_recv()
    dn_share.wait_recv()
    inverse_root = 1.0 / math.sqrt(tokens)
    att_shares[0].wait_recv()

    def left(b):
        total = dot(dm_rows[core, b], att_l[...], NN)
        return (total + dot(dm_sib[b], att_l_sib[...], NN)) * inverse_root

    def right(j):
        total = dot(dn_rows[core, j], att_r[...], NN)
        return ((total + dot(dn_sib[j], att_r_sib[...], NN)) * inverse_root).astype(BF16)

    x_copies = {}

    def send_left(step):
        to = lax.rem(x + step, 4)
        a_send[step] = left(to).astype(BF16)
        x_copies[step] = remote(
            a_send.at[step], a_rec.at[step], a_ssem.at[step], a_rsem.at[step], at(x_=to)
        )
        x_copies[step].start()

    def send_right(step):
        to = lax.rem(y + step, n_y)
        b_send[step] = right(to)
        remote(b_send.at[step], b_rec.at[y], r_send.at[0], r_recv.at[0], at(y_=to)).start()

    order_y = [4, 3, 5, 2, 6, 1, 7] if n_y == 8 else list(range(1, n_y))
    send_left(2)
    att_shares[1].wait_recv()
    for turn, step in enumerate(order_y):
        if turn == 2:
            send_left(1)
        if turn == 4:
            send_left(3)
        send_right(step)
    for step in (1, 3):
        if step not in x_copies:
            send_left(step)
    a_own[...] = left(x)
    b_rec[y] = right(y)

    def settled(src, dst, count, which):
        return remote(
            src.at[pl.ds(0, count)],
            dst.at[pl.ds(0, count)],
            r_send.at[which],
            r_recv.at[which],
            sibling,
        )

    b_all = settled(b_send, b_rec, n_y - 1, 0)

    for h in range(ahead_heads, HEADS):
        scored(h)
    gq_send[...] = wide[...].reshape(peers, group, width).astype(BF16)
    spread(4, gq_send, gq_out)
    gk_send[...] = wide2[...].reshape(peers, group, width).astype(BF16)
    spread(5, gk_send, gk_out, 1, peers // 2)

    mixed = dot(att_l[...], w_full[:, :cols], NT) + dot(att_r[...], w_full[:, cols:], NT)
    mixed = (mixed.reshape(peers, group, width) * gate[None]).astype(BF16)
    for c in range(2):
        branch_out[c] = mixed[:, c * (group // 2) : (c + 1) * (group // 2), :]

    for step in (1, 3, 2):
        x_copies[step].wait()
    total = a_own[...]
    for step in range(1, 4):
        total += a_rec[step].astype(F32)
    a_own[...] = total
    for j in range(n_z):
        a_part[j, :half, :] = a_own[j * half : (j + 1) * half, :].astype(BF16)
    for step in order_y:
        to = lax.rem(y + step, n_y)
        remote(a_part.at[to], a_got.at[y], r_send.at[1], r_recv.at[1], at(y_=to)).start()
    a_got[y] = a_part[y]
    b_all.wait_recv()
    total = b_rec[0].astype(F32)
    for j in range(1, n_y):
        total += b_rec[j].astype(F32)
    b_own[...] = total
    for b in range(4):
        b_part[b, :half, :] = b_own[b * half : (b + 1) * half, :].astype(BF16)
    for step in (2, 1, 3):
        to = lax.rem(x + step, 4)
        remote(b_part.at[to], b_got.at[x], r_send.at[2], r_recv.at[2], at(x_=to)).start()
    b_got[x] = b_part[x]
    b_last = settled(b_part, b_got, 3, 2)
    a_last = settled(a_part, a_got, n_y - 1, 1)
    b_last.wait_recv()
    total = b_got[0].astype(F32)
    for j in range(1, 4):
        total += b_got[j].astype(F32)
    c_send[:, cols:] = total.astype(BF16)
    a_last.wait_recv()
    total = a_got[0].astype(F32)
    for j in range(1, n_y):
        total += a_got[j].astype(F32)
    c_send[:, :cols] = total.astype(BF16)

    owner = y == z
    to_owner = remote(c_send, c_rec.at[z], r_send.at[3], r_recv.at[3], at(z_=y))

    @pl.when(jnp.logical_not(owner))
    def _():
        to_owner.start()

    spread(5, gk_send, gk_out, peers // 2, peers)

    def hand(step):
        return remote(
            fin.at[x_hi],
            fin.at[x_hi],
            r_send.at[4],
            fin_recv.at[x_hi],
            (lax.rem(dp + step, n_dp), seq),
        )

    @pl.when(owner)
    def _():
        c_rec[z] = c_send[...]
        part = c_rec.at[pl.ds(0, n_z - 1)]
        remote(part, part, r_send.at[3], r_recv.at[3], sibling).wait_recv()
        total = c_rec[0].astype(F32)
        for j in range(1, n_z):
            total += c_rec[j].astype(F32)
        fin[x_hi] = total.astype(BF16)

        def send(step, carry):
            hand(step).start()
            return carry

        lax.fori_loop(1, n_dp, send, 0)

    def half_come(which):
        part = fin.at[which]
        return remote(part, part, r_send.at[4], fin_recv.at[which], sibling)

    half_come(1 - x_hi).wait_recv()

    @pl.when(jnp.logical_not(owner))
    def _():
        half_come(x_hi).wait_recv()

    gw_out[:half, :] = fin[0].astype(F32)[:half, :]
    gw_out[half:, :] = fin[1].astype(F32)[:half, :]

    arrive(3, gv_send, gv_out)
    arrive(4, gq_send, gq_out)
    arrive(5, gk_send, gk_out)
    sent(0, q_pl, q_rec)
    sent(1, k_pl, k_rec)
    sent(2, v_pl, v_rec)
    sent(3, gv_send, gv_out)
    sent(4, gq_send, gq_out)
    sent(5, gk_send, gk_out)
    row_sent = w_rec.at[core, x_lo, pl.ds(0, n_y - 1)]
    remote(row_sent, row_sent, w_send.at[1], w_recv.at[1], sibling).wait_send()
    all_sent = w_rec.at[core, x_lo]
    remote(all_sent, all_sent, w_send.at[2], w_recv.at[1], sibling).wait_send()
    remote(w_rec.at[core], w_rec.at[core], w_send.at[3], w_recv.at[1], sibling).wait_send()
    dm_share.wait_send()
    for copy in att_shares:
        copy.wait_send()
    dn_share.wait_send()
    b_all.wait_send()
    a_last.wait_send()
    b_last.wait_send()

    @pl.when(jnp.logical_not(owner))
    def _():
        to_owner.wait_send()

    @pl.when(owner)
    def _():
        def sent_on(step, carry):
            hand(step).wait_send()
            return carry

        lax.fori_loop(1, n_dp, sent_on, 0)


def settle(
    branch_in,
    gq_in,
    gk_in,
    gv_in,
    gw_in,
    branch_out,
    gq_out,
    gk_out,
    gv_out,
    gw_out,
    gq_pl,
    gk_pl,
    gv_pl,
    gq_own,
    gk_own,
    gv_own,
    branch_own,
    gw_own,
    sem,
):
    copies = [
        pltpu.make_async_copy(src, dst, sem.at[i])
        for i, (src, dst) in enumerate(
            (
                (gv_in, gv_pl),
                (gq_in, gq_pl),
                (gk_in, gk_pl),
                (branch_in, branch_own),
                (gw_in, gw_own),
            )
        )
    ]
    for copy in copies:
        copy.start()
    triples = ((gv_pl, gv_own, gv_out), (gq_pl, gq_own, gq_out), (gk_pl, gk_own, gk_out))
    for i, (src, own, dst) in enumerate(triples):
        peers, group, width = src.shape
        each = group // 2
        copies[i].wait()
        pairs = src[...].astype(F32).reshape(peers // 2, 2, group, width)
        even, odd = pairs[:, 0], pairs[:, 1]
        for c in range(2):
            part = slice(c * each, (c + 1) * each)
            both = jnp.concatenate([even[:, part], odd[:, part]], axis=1)
            own[c, 0] = both.reshape(peers * each, width).astype(BF16)
        copies.append(pltpu.make_async_copy(own, dst, sem.at[5 + i]))
        copies[-1].start()
    for i, (own, dst) in ((3, (branch_own, branch_out)), (4, (gw_own, gw_out))):
        copies[i].wait()
        copies.append(pltpu.make_async_copy(own, dst, sem.at[5 + i]))
        copies[-1].start()
    for copy in copies[5:]:
        copy.wait()


def body(n_y, n_z, tokens, queries, key_states, value_states, gate_vector, out_weight, cotangent):
    clips, frames, patches, width = cotangent.shape
    group, rows = clips * patches, clips * patches * frames
    own_rows = out_weight.shape[0]
    half = own_rows // 2
    block, tall, pad = n_z * half, 4 * half, up8(half)
    cols = (width // 128 + 1) // 2 * 128

    plane = jax.ShapeDtypeStruct((frames, group, width), BF16)
    vmem = pl.BlockSpec(memory_space=pltpu.VMEM)
    flat = pltpu.VMEM((rows, width), BF16)
    flat32 = pltpu.VMEM((rows, width), F32)
    stack = pltpu.VMEM((frames, group, width), BF16)
    dma = pltpu.SemaphoreType.DMA
    branch, gq, gk, gv, gw = pl.pallas_call(
        functools.partial(kernel, n_y, n_z, tokens),
        out_shape=[
            jax.ShapeDtypeStruct(cotangent.shape, BF16),
            plane,
            plane,
            plane,
            jax.ShapeDtypeStruct((own_rows, width), F32),
        ],
        in_specs=[vmem] * 6,
        out_specs=[vmem] * 5,
        scratch_shapes=[
            stack,
            stack,
            stack,
            flat,
            stack,
            stack,
            stack,
            flat,
            flat,
            flat,
            pltpu.VMEM((2, 2, n_z, own_rows, width), BF16),
            pltpu.VMEM((width, width), BF16),
            pltpu.VMEM((rows, rows), F32),
            pltpu.VMEM((HEADS, rows, rows), F32),
            flat,
            flat32,
            flat32,
            stack,
            stack,
            stack,
            pltpu.VMEM((2, 4, block, rows), BF16),
            pltpu.VMEM((4, block, rows), BF16),
            pltpu.VMEM((HEADS, rows, rows), BF16),
            pltpu.VMEM((rows, cols), BF16),
            pltpu.VMEM((rows, width - cols), BF16),
            pltpu.VMEM((rows, cols), BF16),
            pltpu.VMEM((rows, width - cols), BF16),
            pltpu.VMEM((2, n_z, tall, rows), BF16),
            pltpu.VMEM((n_z, tall, rows), BF16),
            pltpu.VMEM((block, cols), F32),
            pltpu.VMEM((4, block, cols), BF16),
            pltpu.VMEM((4, block, cols), BF16),
            pltpu.VMEM((n_z, pad, cols), BF16),
            pltpu.VMEM((n_y, pad, cols), BF16),
            pltpu.VMEM((tall, width - cols), F32),
            pltpu.VMEM((n_y, tall, width - cols), BF16),
            pltpu.VMEM((n_y, tall, width - cols), BF16),
            pltpu.VMEM((4, pad, width - cols), BF16),
            pltpu.VMEM((4, pad, width - cols), BF16),
            pltpu.VMEM((pad, width), BF16),
            pltpu.VMEM((n_z, pad, width), BF16),
            pltpu.VMEM((2, pad, width), BF16),
            dma((6,)),
            dma((6,)),
            dma((6,)),
            dma((4,)),
            dma((3,)),
            dma((n_y,)),
            dma((n_y,)),
            dma((4,)),
            dma((4,)),
            dma((4,)),
            dma((4,)),
            dma((5,)),
            dma((5,)),
            dma((2,)),
        ],
        compiler_params=pltpu.CompilerParams(
            collective_id=1, has_side_effects=True, vmem_limit_bytes=56 << 20
        ),
    )(queries, key_states, value_states, cotangent, gate_vector, out_weight)

    whole = pl.BlockSpec(memory_space=pltpu.HBM)
    own = pltpu.VMEM(queries.shape, BF16)
    return pl.pallas_call(
        settle,
        out_shape=[
            jax.ShapeDtypeStruct(branch.shape, branch.dtype),
            jax.ShapeDtypeStruct(queries.shape, BF16),
            jax.ShapeDtypeStruct(queries.shape, BF16),
            jax.ShapeDtypeStruct(queries.shape, BF16),
            jax.ShapeDtypeStruct(gw.shape, gw.dtype),
        ],
        in_specs=[whole] * 5,
        out_specs=[whole] * 5,
        scratch_shapes=[
            stack,
            stack,
            stack,
            own,
            own,
            own,
            pltpu.VMEM(branch.shape, branch.dtype),
            pltpu.VMEM(gw.shape, gw.dtype),
            dma((10,)),
        ],
        compiler_params=pltpu.CompilerParams(vmem_limit_bytes=60 << 20),
    )(branch, gq, gk, gv, gw)


def solution(mesh):
    n_dp, n_seq = mesh.shape["dp"], mesh.shape["seq"]

    def step(queries, key_states, value_states, gate_vector, out_weight, cotangent):
        clips, frames, patches, _ = cotangent.shape
        tokens = clips * frames * patches * n_dp * n_seq
        return body(
            n_dp // 2,
            n_seq // 4,
            tokens,
            queries,
            key_states,
            value_states,
            gate_vector,
            out_weight,
            cotangent,
        )

    framed = P("dp", "seq", None, None)
    patched = P("dp", None, "seq", None)
    return jax.shard_map(
        step,
        mesh=mesh,
        in_specs=(framed, framed, framed, P("dp", None), P("seq", None), patched),
        out_specs=(patched, framed, framed, framed, P("seq", None)),
        check_vma=False,
    )
```

```python
import functools
import math

import jax
import jax.numpy as jnp
from jax import lax
from jax.experimental import pallas as pl
from jax.experimental.pallas import tpu as pltpu
from jax.sharding import PartitionSpec as P

HEADS = 16
MESH = pl.DeviceIdType.MESH
F32 = jnp.float32
BF16 = jnp.bfloat16
NT = (((1,), (1,)), ((), ()))
NN = (((1,), (0,)), ((), ()))
TN = (((0,), (0,)), ((), ()))


def dot(a, b, dims):
    return lax.dot_general(a, b, dims, preferred_element_type=F32)


def up8(n):
    return -(-n // 8) * 8


def kernel(
    n_y,
    n_z,
    tokens,
    q_in,
    k_in,
    v_in,
    cot_in,
    gate_in,
    w_in,
    branch_out,
    gq_out,
    gk_out,
    gv_out,
    gw_out,
    q_raw,
    k_raw,
    v_raw,
    cot_raw,
    in_sem,
    q_pl,
    k_pl,
    v_pl,
    d_mix,
    q_rec,
    k_rec,
    v_rec,
    q_rows,
    k_rows,
    v_rows,
    w_rec,
    w_full,
    bias,
    probs,
    d_att,
    wide,
    wide2,
    gq_send,
    gk_send,
    gv_send,
    dm_rows,
    dm_sib,
    p_turn,
    att_l,
    att_r,
    att_l_sib,
    att_r_sib,
    dn_rows,
    dn_sib,
    a_own,
    a_send,
    a_rec,
    a_part,
    a_got,
    b_own,
    b_send,
    b_rec,
    b_part,
    b_got,
    c_send,
    c_rec,
    fin,
    a2a_send,
    a2a_recv,
    a2a_own,
    w_send,
    w_recv,
    wy_recv,
    wx_recv,
    sib_send,
    sib_recv,
    a_ssem,
    a_rsem,
    r_send,
    r_recv,
    fin_recv,
):
    peers, group, width = q_rec.shape
    rows = peers * group
    head = width // HEADS
    scale = 1.0 / math.sqrt(head)
    own_rows = w_in.shape[0]
    half = own_rows // 2
    dp, seq = lax.axis_index("dp"), lax.axis_index("seq")
    y, x_hi = lax.div(dp, 2), lax.rem(dp, 2)
    core, z, x_lo = lax.rem(seq, 2), lax.rem(lax.div(seq, 2), n_z), lax.div(seq, 2 * n_z)
    x = 2 * x_hi + x_lo

    def at(y_=None, x_=None, z_=None, core_=None):
        y_ = y if y_ is None else y_
        x_ = x if x_ is None else x_
        z_ = z if z_ is None else z_
        core_ = core if core_ is None else core_
        return (2 * y_ + lax.div(x_, 2), (lax.rem(x_, 2) * n_z + z_) * 2 + core_)

    def remote(src, dst, send, recv, to):
        return pltpu.make_async_remote_copy(
            src_ref=src,
            dst_ref=dst,
            send_sem=send,
            recv_sem=recv,
            device_id=to,
            device_id_type=MESH,
        )

    sibling = at(core_=1 - core)
    ahead, behind = at(x_=lax.rem(x + 1, 4)), at(x_=lax.rem(x + 3, 4))

    fetches = [
        pltpu.make_async_copy(src, dst, in_sem.at[i])
        for i, (src, dst) in enumerate(
            ((q_in, q_raw), (k_in, k_raw), (v_in, v_raw), (cot_in, cot_raw))
        )
    ]
    for copy in fetches:
        copy.start()

    barrier = pltpu.get_barrier_semaphore()

    def greet(to):
        pl.semaphore_signal(barrier, inc=1, device_id=to, device_id_type=MESH)

    def greet_seq(step, carry):
        greet((dp, lax.rem(seq + step, peers)))
        return carry

    lax.fori_loop(1, peers, greet_seq, 0)
    n_dp = 2 * n_y

    def greet_dp(step, carry):
        greet((lax.rem(dp + step, n_dp), seq))
        return carry

    lax.fori_loop(1, n_dp, greet_dp, 0)
    greet(at(x_=2 * (1 - x_hi) + 1 - x_lo))
    def deal(src, dst):
        first = src[0, 0].astype(F32).reshape(peers // 2, group, width)
        second = src[1, 0].astype(F32).reshape(peers // 2, group, width)
        each = group // 2
        even = jnp.concatenate([first[:, :each], second[:, :each]], axis=1)
        odd = jnp.concatenate([first[:, each:], second[:, each:]], axis=1)
        both = jnp.stack([even, odd], axis=1).reshape(peers, group, width)
        dst[...] = both.astype(BF16)

    for i, (raw, planes) in enumerate(((q_raw, q_pl), (k_raw, k_pl), (v_raw, v_pl))):
        fetches[i].wait()
        deal(raw, planes)
    pl.semaphore_wait(barrier, peers + n_dp - 1)

    slot = lax.rem(z + y, n_z)
    w_first = remote(
        w_in,
        w_rec.at[core, x_lo, z],
        w_send.at[0],
        w_recv.at[0],
        at(z_=lax.rem(z - y + n_z, n_z)),
    )
    w_own = pltpu.make_async_copy(w_in, w_rec.at[core, x_lo, z], w_recv.at[2])

    @pl.when(y != 0)
    def _():
        w_first.start()

    @pl.when(y == 0)
    def _():
        w_own.start()

    def spread(t, src, dst, first=1, last=None):
        def send(step, carry):
            target = lax.rem(seq + step, peers)
            remote(
                src.at[target], dst.at[seq], a2a_send.at[t], a2a_recv.at[t], (dp, target)
            ).start()
            return carry

        lax.fori_loop(first, last or peers, send, 0)
        if first == 1:
            pltpu.make_async_copy(src.at[seq], dst.at[seq], a2a_own.at[t]).start()

    def arrive(t, src, dst):
        remote(
            src.at[pl.ds(0, peers - 1)],
            dst.at[pl.ds(0, peers - 1)],
            a2a_send.at[t],
            a2a_recv.at[t],
            sibling,
        ).wait_recv()
        pltpu.make_async_copy(src.at[seq], dst.at[seq], a2a_own.at[t]).wait()

    def sent(t, src, dst):
        remote(
            src.at[pl.ds(0, peers - 1)],
            dst.at[pl.ds(0, peers - 1)],
            a2a_send.at[t],
            a2a_recv.at[t],
            sibling,
        ).wait_send()

    spread(0, q_pl, q_rec)
    spread(1, k_pl, k_rec)
    spread(2, v_pl, v_rec)

    @pl.when(y != 0)
    def _():
        w_first.wait()

    @pl.when(y == 0)
    def _():
        w_own.wait()

    order = [1, 7, 2, 6, 3, 5, 4][:n_y - 1] if n_y == 8 else list(range(1, n_y))

    def shard(step, x_lo_):
        return w_rec.at[core, x_lo_, lax.rem(z + y - step + n_z, n_z)]

    def hop(step, x_lo_, send, recv, to):
        return remote(shard(step, x_lo_), shard(step, x_lo_), send, recv, to)

    def along_y(step):
        return hop(step, x_lo, w_send.at[1], wy_recv.at[step], sibling)

    def along_x(step, turn, x_lo_):
        to = ahead if turn % 2 else behind
        return hop(step, x_lo_, w_send.at[2], wx_recv.at[step], to)

    def across(step, x_lo_):
        return hop(step, x_lo_, w_send.at[3], w_recv.at[1], sibling)

    for step in order:
        remote(
            shard(0, x_lo),
            shard(0, x_lo),
            w_send.at[1],
            wy_recv.at[step],
            at(y_=lax.rem(y + step, n_y)),
        ).start()
    along_x(0, 0, x_lo).start()
    across(0, x_lo).start()

    gate = jnp.concatenate(
        [jnp.broadcast_to(gate_in[c : c + 1, :], (group // 2, width)) for c in range(2)], axis=0
    )
    fetches[3].wait()
    cot = jnp.concatenate([cot_raw[0].astype(F32), cot_raw[1].astype(F32)], axis=1)
    d_mix[...] = (cot * gate[None]).reshape(rows, width).astype(BF16)
    block, tall = n_z * half, 4 * half
    far = n_z * 2 * own_rows

    def picked(row, first):
        lane = lax.broadcasted_iota(jnp.int32, (row.shape[0], width), 1)
        pick = (lane == row + first).astype(F32).astype(BF16)
        return dot(pick, d_mix[...], NT).astype(BF16)

    def by_x(c):
        row = lax.broadcasted_iota(jnp.int32, (block, 1), 0)
        turn = sum((row >= half * j).astype(jnp.int32) for j in range(1, n_z))
        row = row + turn * (2 * own_rows - half)
        for b in range(4):
            dm_rows[c, b] = picked(row, (b % 2) * far + c * own_rows + (b // 2) * half)

    def by_z(c):
        row = lax.broadcasted_iota(jnp.int32, (tall, 1), 0)
        turn = sum((row >= half * j).astype(jnp.int32) for j in range(1, 4))
        upper = (row >= half * 2).astype(jnp.int32)
        row = row - turn * half + upper * half + (turn - 2 * upper) * far
        for j in range(n_z):
            dn_rows[c, j] = picked(row, j * 2 * own_rows + c * own_rows)

    def clear():
        row_of = lax.broadcasted_iota(jnp.int32, (rows, rows), 0)
        col_of = lax.broadcasted_iota(jnp.int32, (rows, rows), 1)
        bias[...] = jnp.where(lax.rem(row_of, group) == lax.rem(col_of, group), 0.0, -1e30)
        a_part[...] = jnp.zeros_like(a_part)
        b_part[...] = jnp.zeros_like(b_part)

    dm_share = remote(
        dm_rows.at[1 - core], dm_sib, sib_send.at[0], sib_recv.at[0], sibling
    )
    dn_share = remote(
        dn_rows.at[1 - core], dn_sib, sib_send.at[2], sib_recv.at[2], sibling
    )
    chores = [
        lambda: by_x(0),
        lambda: by_x(1),
        dm_share.start,
        lambda: by_z(0),
        lambda: by_z(1),
        dn_share.start,
        clear,
    ]
    for turn, step in enumerate(order, 1):
        along_y(step).wait_recv()
        along_x(step, turn, x_lo).start()
        across(step, x_lo).start()
        if chores:
            chores.pop(0)()
    for chore in chores:
        chore()
    for turn, step in enumerate([0] + order):
        along_x(step, turn, 1 - x_lo).wait_recv()
        across(step, 1 - x_lo).start()

    def to_rows(dst, src):
        dst[...] = src[...].astype(F32).reshape(rows, width).astype(BF16)

    def cut(ref, h):
        return ref[:, h * head : (h + 1) * head]

    def softmax(h):
        score = dot(cut(k_rows, h), cut(q_rows, h), NT) + bias[...]
        top = jnp.max(score, axis=0, keepdims=True)
        grown = jnp.exp((score - top) * scale)
        probs[h] = grown * (1.0 / jnp.sum(grown, axis=0, keepdims=True))

    arrive(0, q_pl, q_rec)
    arrive(1, k_pl, k_rec)
    to_rows(q_rows, q_rec)
    to_rows(k_rows, k_rec)
    for h in range(HEADS):
        softmax(h)
    remote(
        w_rec.at[core], w_rec.at[1 - core], w_send.at[3], w_recv.at[1], sibling
    ).wait_recv()

    quad = 4 * own_rows
    for b in range(peers // 4):
        parts = []
        for s in range(4 * b, 4 * b + 4):
            parts.append(w_rec[s % 2, s // (2 * n_z), (s // 2) % n_z].astype(F32))
        w_full[b * quad : (b + 1) * quad, :] = jnp.concatenate(parts, axis=0).astype(BF16)
    d_att[...] = dot(d_mix[...], w_full[...], NN).astype(BF16)
    for h in range(HEADS):
        wide[:, h * head : (h + 1) * head] = dot(probs[h].astype(BF16), cut(d_att, h), NN)
    gv_send[...] = wide[...].reshape(peers, group, width).astype(BF16)
    spread(3, gv_send, gv_out)

    for h in range(HEADS):
        p_turn[h] = probs[h].T.astype(BF16)

    cols = (width // 128 + 1) // 2 * 128
    left_heads = -(-cols // head)
    att_shares = (
        remote(att_l, att_l_sib, sib_send.at[1], sib_recv.at[1], sibling),
        remote(att_r, att_r_sib, sib_send.at[3], sib_recv.at[3], sibling),
    )
    arrive(2, v_pl, v_rec)
    to_rows(v_rows, v_rec)
    for h in range(left_heads):
        wide[:, h * head : (h + 1) * head] = dot(p_turn[h], cut(v_rows, h), NN)
    att_l[...] = wide[:, :cols].astype(BF16)
    att_shares[0].start()
    for h in range(left_heads, HEADS):
        wide[:, h * head : (h + 1) * head] = dot(p_turn[h], cut(v_rows, h), NN)
    att_r[...] = wide[:, cols:].astype(BF16)
    att_shares[1].start()

    def scored(h):
        prob = probs[h]
        d_prob = dot(cut(v_rows, h), cut(d_att, h), NT)
        centre = jnp.sum(prob * d_prob, axis=0, keepdims=True)
        d_score = (prob * (d_prob - centre) * scale).astype(BF16)
        wide[:, h * head : (h + 1) * head] = dot(d_score, cut(k_rows, h), TN)
        wide2[:, h * head : (h + 1) * head] = dot(d_score, cut(q_rows, h), NN)

    ahead_heads = HEADS // 4
    for h in range(ahead_heads):
        scored(h)

    dm_share.wait_recv()
    dn_share.wait_recv()
    inverse_root = 1.0 / math.sqrt(tokens)
    att_shares[0].wait_recv()

    def left(b):
        total = dot(dm_rows[core, b], att_l[...], NN)
        return (total + dot(dm_sib[b], att_l_sib[...], NN)) * inverse_root

    def right(j):
        total = dot(dn_rows[core, j], att_r[...], NN)
        return ((total + dot(dn_sib[j], att_r_sib[...], NN)) * inverse_root).astype(BF16)

    x_copies = {}

    def send_left(step):
        to = lax.rem(x + step, 4)
        a_send[step] = left(to).astype(BF16)
        x_copies[step] = remote(
            a_send.at[step], a_rec.at[step], a_ssem.at[step], a_rsem.at[step], at(x_=to)
        )
        x_copies[step].start()

    def send_right(step):
        to = lax.rem(y + step, n_y)
        b_send[step] = right(to)
        remote(b_send.at[step], b_rec.at[y], r_send.at[0], r_recv.at[0], at(y_=to)).start()

    order_y = [4, 3, 5, 2, 6, 1, 7] if n_y == 8 else list(range(1, n_y))
    send_left(2)
    att_shares[1].wait_recv()
    for turn, step in enumerate(order_y):
        if turn == 2:
            send_left(1)
        if turn == 4:
            send_left(3)
        send_right(step)
    for step in (1, 3):
        if step not in x_copies:
            send_left(step)
    a_own[...] = left(x)
    b_rec[y] = right(y)

    def settled(src, dst, count, which):
        return remote(
            src.at[pl.ds(0, count)],
            dst.at[pl.ds(0, count)],
            r_send.at[which],
            r_recv.at[which],
            sibling,
        )

    b_all = settled(b_send, b_rec, n_y - 1, 0)

    for h in range(ahead_heads, HEADS):
        scored(h)
    gq_send[...] = wide[...].reshape(peers, group, width).astype(BF16)
    spread(4, gq_send, gq_out)
    gk_send[...] = wide2[...].reshape(peers, group, width).astype(BF16)
    spread(5, gk_send, gk_out, 1, peers // 2)

    mixed = dot(att_l[...], w_full[:, :cols], NT) + dot(att_r[...], w_full[:, cols:], NT)
    mixed = (mixed.reshape(peers, group, width) * gate[None]).astype(BF16)
    for c in range(2):
        branch_out[c] = mixed[:, c * (group // 2) : (c + 1) * (group // 2), :]

    for step in (1, 3, 2):
        x_copies[step].wait()
    total = a_own[...]
    for step in range(1, 4):
        total += a_rec[step].astype(F32)
    a_own[...] = total
    for j in range(n_z):
        a_part[j, :half, :] = a_own[j * half : (j + 1) * half, :].astype(BF16)
    for step in order_y:
        to = lax.rem(y + step, n_y)
        remote(a_part.at[to], a_got.at[y], r_send.at[1], r_recv.at[1], at(y_=to)).start()
    a_got[y] = a_part[y]
    b_all.wait_recv()
    total = b_rec[0].astype(F32)
    for j in range(1, n_y):
        total += b_rec[j].astype(F32)
    b_own[...] = total
    for b in range(4):
        b_part[b, :half, :] = b_own[b * half : (b + 1) * half, :].astype(BF16)
    for step in (2, 1, 3):
        to = lax.rem(x + step, 4)
        remote(b_part.at[to], b_got.at[x], r_send.at[2], r_recv.at[2], at(x_=to)).start()
    b_got[x] = b_part[x]
    b_last = settled(b_part, b_got, 3, 2)
    a_last = settled(a_part, a_got, n_y - 1, 1)
    b_last.wait_recv()
    total = b_got[0].astype(F32)
    for j in range(1, 4):
        total += b_got[j].astype(F32)
    c_send[:, cols:] = total.astype(BF16)
    a_last.wait_recv()
    total = a_got[0].astype(F32)
    for j in range(1, n_y):
        total += a_got[j].astype(F32)
    c_send[:, :cols] = total.astype(BF16)

    owner = y == z
    to_owner = remote(c_send, c_rec.at[z], r_send.at[3], r_recv.at[3], at(z_=y))

    @pl.when(jnp.logical_not(owner))
    def _():
        to_owner.start()

    spread(5, gk_send, gk_out, peers // 2, peers)

    def hand(step):
        return remote(
            fin.at[x_hi],
            fin.at[x_hi],
            r_send.at[4],
            fin_recv.at[x_hi],
            (lax.rem(dp + step, n_dp), seq),
        )

    @pl.when(owner)
    def _():
        c_rec[z] = c_send[...]
        part = c_rec.at[pl.ds(0, n_z - 1)]
        remote(part, part, r_send.at[3], r_recv.at[3], sibling).wait_recv()
        total = c_rec[0].astype(F32)
        for j in range(1, n_z):
            total += c_rec[j].astype(F32)
        fin[x_hi] = total.astype(BF16)

        def send(step, carry):
            hand(step).start()
            return carry

        lax.fori_loop(1, n_dp, send, 0)

    def half_come(which):
        part = fin.at[which]
        return remote(part, part, r_send.at[4], fin_recv.at[which], sibling)

    half_come(1 - x_hi).wait_recv()

    @pl.when(jnp.logical_not(owner))
    def _():
        half_come(x_hi).wait_recv()

    gw_out[:half, :] = fin[0].astype(F32)[:half, :]
    gw_out[half:, :] = fin[1].astype(F32)[:half, :]

    arrive(3, gv_send, gv_out)
    arrive(4, gq_send, gq_out)
    arrive(5, gk_send, gk_out)
    sent(0, q_pl, q_rec)
    sent(1, k_pl, k_rec)
    sent(2, v_pl, v_rec)
    sent(3, gv_send, gv_out)
    sent(4, gq_send, gq_out)
    sent(5, gk_send, gk_out)
    row_sent = w_rec.at[core, x_lo, pl.ds(0, n_y - 1)]
    remote(row_sent, row_sent, w_send.at[1], w_recv.at[1], sibling).wait_send()
    all_sent = w_rec.at[core, x_lo]
    remote(all_sent, all_sent, w_send.at[2], w_recv.at[1], sibling).wait_send()
    remote(w_rec.at[core], w_rec.at[core], w_send.at[3], w_recv.at[1], sibling).wait_send()
    dm_share.wait_send()
    for copy in att_shares:
        copy.wait_send()
    dn_share.wait_send()
    b_all.wait_send()
    a_last.wait_send()
    b_last.wait_send()

    @pl.when(jnp.logical_not(owner))
    def _():
        to_owner.wait_send()

    @pl.when(owner)
    def _():
        def sent_on(step, carry):
            hand(step).wait_send()
            return carry

        lax.fori_loop(1, n_dp, sent_on, 0)


def settle(
    branch_in,
    gq_in,
    gk_in,
    gv_in,
    gw_in,
    branch_out,
    gq_out,
    gk_out,
    gv_out,
    gw_out,
    gq_pl,
    gk_pl,
    gv_pl,
    gq_own,
    gk_own,
    gv_own,
    branch_own,
    gw_own,
    sem,
):
    copies = [
        pltpu.make_async_copy(src, dst, sem.at[i])
        for i, (src, dst) in enumerate(
            (
                (gv_in, gv_pl),
                (gq_in, gq_pl),
                (gk_in, gk_pl),
                (branch_in, branch_own),
                (gw_in, gw_own),
            )
        )
    ]
    for copy in copies:
        copy.start()
    triples = ((gv_pl, gv_own, gv_out), (gq_pl, gq_own, gq_out), (gk_pl, gk_own, gk_out))
    for i, (src, own, dst) in enumerate(triples):
        peers, group, width = src.shape
        each = group // 2
        copies[i].wait()
        pairs = src[...].astype(F32).reshape(peers // 2, 2, group, width)
        even, odd = pairs[:, 0], pairs[:, 1]
        for c in range(2):
            part = slice(c * each, (c + 1) * each)
            both = jnp.concatenate([even[:, part], odd[:, part]], axis=1)
            own[c, 0] = both.reshape(peers * each, width).astype(BF16)
        copies.append(pltpu.make_async_copy(own, dst, sem.at[5 + i]))
        copies[-1].start()
    for i, (own, dst) in ((3, (branch_own, branch_out)), (4, (gw_own, gw_out))):
        copies[i].wait()
        copies.append(pltpu.make_async_copy(own, dst, sem.at[5 + i]))
        copies[-1].start()
    for copy in copies[5:]:
        copy.wait()


def body(n_y, n_z, tokens, queries, key_states, value_states, gate_vector, out_weight, cotangent):
    clips, frames, patches, width = cotangent.shape
    group, rows = clips * patches, clips * patches * frames
    own_rows = out_weight.shape[0]
    half = own_rows // 2
    block, tall, pad = n_z * half, 4 * half, up8(half)
    cols = (width // 128 + 1) // 2 * 128

    plane = jax.ShapeDtypeStruct((frames, group, width), BF16)
    vmem = pl.BlockSpec(memory_space=pltpu.VMEM)
    hbm = pl.BlockSpec(memory_space=pltpu.HBM)
    own = pltpu.VMEM(queries.shape, BF16)
    flat = pltpu.VMEM((rows, width), BF16)
    flat32 = pltpu.VMEM((rows, width), F32)
    stack = pltpu.VMEM((frames, group, width), BF16)
    dma = pltpu.SemaphoreType.DMA
    branch, gq, gk, gv, gw = pl.pallas_call(
        functools.partial(kernel, n_y, n_z, tokens),
        out_shape=[
            jax.ShapeDtypeStruct(cotangent.shape, BF16),
            plane,
            plane,
            plane,
            jax.ShapeDtypeStruct((own_rows, width), F32),
        ],
        in_specs=[hbm] * 4 + [vmem] * 2,
        out_specs=[vmem] * 5,
        scratch_shapes=[
            own,
            own,
            own,
            pltpu.VMEM(cotangent.shape, BF16),
            dma((4,)),
            stack,
            stack,
            stack,
            flat,
            stack,
            stack,
            stack,
            flat,
            flat,
            flat,
            pltpu.VMEM((2, 2, n_z, own_rows, width), BF16),
            pltpu.VMEM((width, width), BF16),
            pltpu.VMEM((rows, rows), F32),
            pltpu.VMEM((HEADS, rows, rows), F32),
            flat,
            flat32,
            flat32,
            stack,
            stack,
            stack,
            pltpu.VMEM((2, 4, block, rows), BF16),
            pltpu.VMEM((4, block, rows), BF16),
            pltpu.VMEM((HEADS, rows, rows), BF16),
            pltpu.VMEM((rows, cols), BF16),
            pltpu.VMEM((rows, width - cols), BF16),
            pltpu.VMEM((rows, cols), BF16),
            pltpu.VMEM((rows, width - cols), BF16),
            pltpu.VMEM((2, n_z, tall, rows), BF16),
            pltpu.VMEM((n_z, tall, rows), BF16),
            pltpu.VMEM((block, cols), F32),
            pltpu.VMEM((4, block, cols), BF16),
            pltpu.VMEM((4, block, cols), BF16),
            pltpu.VMEM((n_z, pad, cols), BF16),
            pltpu.VMEM((n_y, pad, cols), BF16),
            pltpu.VMEM((tall, width - cols), F32),
            pltpu.VMEM((n_y, tall, width - cols), BF16),
            pltpu.VMEM((n_y, tall, width - cols), BF16),
            pltpu.VMEM((4, pad, width - cols), BF16),
            pltpu.VMEM((4, pad, width - cols), BF16),
            pltpu.VMEM((pad, width), BF16),
            pltpu.VMEM((n_z, pad, width), BF16),
            pltpu.VMEM((2, pad, width), BF16),
            dma((6,)),
            dma((6,)),
            dma((6,)),
            dma((4,)),
            dma((3,)),
            dma((n_y,)),
            dma((n_y,)),
            dma((4,)),
            dma((4,)),
            dma((4,)),
            dma((4,)),
            dma((5,)),
            dma((5,)),
            dma((2,)),
        ],
        compiler_params=pltpu.CompilerParams(
            collective_id=1, has_side_effects=True, vmem_limit_bytes=56 << 20
        ),
    )(queries, key_states, value_states, cotangent, gate_vector, out_weight)

    return pl.pallas_call(
        settle,
        out_shape=[
            jax.ShapeDtypeStruct(branch.shape, branch.dtype),
            jax.ShapeDtypeStruct(queries.shape, BF16),
            jax.ShapeDtypeStruct(queries.shape, BF16),
            jax.ShapeDtypeStruct(queries.shape, BF16),
            jax.ShapeDtypeStruct(gw.shape, gw.dtype),
        ],
        in_specs=[hbm] * 5,
        out_specs=[hbm] * 5,
        scratch_shapes=[
            stack,
            stack,
            stack,
            own,
            own,
            own,
            pltpu.VMEM(branch.shape, branch.dtype),
            pltpu.VMEM(gw.shape, gw.dtype),
            dma((10,)),
        ],
        compiler_params=pltpu.CompilerParams(vmem_limit_bytes=60 << 20),
    )(branch, gq, gk, gv, gw)


def solution(mesh):
    n_dp, n_seq = mesh.shape["dp"], mesh.shape["seq"]

    def step(queries, key_states, value_states, gate_vector, out_weight, cotangent):
        clips, frames, patches, _ = cotangent.shape
        tokens = clips * frames * patches * n_dp * n_seq
        return body(
            n_dp // 2,
            n_seq // 4,
            tokens,
            queries,
            key_states,
            value_states,
            gate_vector,
            out_weight,
            cotangent,
        )

    framed = P("dp", "seq", None, None)
    patched = P("dp", None, "seq", None)
    return jax.shard_map(
        step,
        mesh=mesh,
        in_specs=(framed, framed, framed, P("dp", None), P("seq", None), patched),
        out_specs=(patched, framed, framed, framed, P("seq", None)),
        check_vma=False,
    )
```
